128 devices in a mesh: group: 8 (over z, core), member: 16 (over x, y).
Axes of the slice: x: 4, y: 4, z: 4, core: 2. Of those that a mesh axis runs over, the one named last changes fastest.
Arguments:
- tokens: bfloat16 [2048, 3584], P(('group', 'member')), may hold values from -6 to 6
- routes: int32 [2048, 8], P(('group', 'member')), may hold values from 0 to 127, all different within a row; in each aligned block of 16 rows (0 to 15, 16 to 31, ...) at most 2 rows name the same one
- affinity: float32 [2048, 8], P(('group', 'member')), may hold values from -8 to 8
- w_gate: bfloat16 [128, 3584, 1024], P(('group', 'member')), may hold values from -0.09375 to 0.09375
- w_up: bfloat16 [128, 3584, 1024], P(('group', 'member')), may hold values from -0.09375 to 0.09375
- w_down: bfloat16 [128, 1024, 3584], P(('group', 'member')), may hold values from -0.1875 to 0.1875
- q_latent: bfloat16 [1024, 64, 512], P(('group', 'member')), may hold values from -6 to 6
- q_rope: bfloat16 [1024, 4096], P(('group', 'member')), may hold values from -60 to 60
- cache_latent: bfloat16 [1024, 256, 512], P(('group', 'member')), may hold values from -6 to 6
- cache_rope: bfloat16 [1024, 64, 256], P(('group', 'member')), may hold values from -6 to 6
- lengths: int32 [1024], P(('group', 'member')), may hold values from 2 to 256, as said below
Outputs:
- moe_out: bfloat16 [2048, 3584], P(('group', 'member'))
- attn_out: bfloat16 [1024, 32768], P(('group', 'member'))
The draws below stay inside these ranges and needn't reach their ends.
Inputs may be any that keep to these rules, and one draw needn't show every extreme that they name: `routes`: each row names 8 different experts; among the rows of one device no expert is named by more than 2 rows. `lengths`: some sequence fills its whole cache.
All inputs are finite; a program needn't handle non-finite values.
Results may differ from the reference program's by a relative error of at most 0.0058.
Values may be sent and summed in bfloat16 or wider, within the bound.
A program may use at most 128 MiB of HBM per device.

```python
import math
import jax
import jax.numpy as jnp
import numpy as np
from jax import lax

D = 3584
FF = 1024
EXPERTS = 128
TOPK = 8
TOK_DEV = 16
TOKENS = 2048
CAP = 2
HEADS = 64
LAT = 512
ROPE = 64
SEQS = 1024
CACHE = 256


def draw_q_rope(key, part):
    key = jax.random.fold_in(key, 11)
    values = jnp.clip(jax.random.normal(key, (SEQS, HEADS, ROPE), jnp.float32), -6.0, 6.0)
    return values.reshape(SEQS, HEADS * ROPE).astype(jnp.bfloat16)


def draw_cache_rope(key, part):
    key = jax.random.fold_in(key, 12)
    values = jnp.clip(jax.random.normal(key, (SEQS, ROPE, CACHE), jnp.float32), -6.0, 6.0)
    return values.astype(jnp.bfloat16)


def draw_lengths(key, part):
    key = jax.random.fold_in(key, 13)
    filled = jax.random.randint(key, (SEQS,), 2, CACHE + 1)
    picked = jax.random.randint(jax.random.fold_in(key, 1), (), 0, SEQS)
    return filled.at[picked].set(CACHE).astype(jnp.int32)


def shard_levels(stream_key, dims, cuts, least, high):
    level = 1.0
    for dim, shards_of in cuts:
        heights = jax.random.uniform(jax.random.fold_in(jax.random.fold_in(stream_key, 6), dim), (shards_of,), jnp.float32, least / len(cuts), high / len(cuts))
        level = level * jnp.repeat(jnp.exp(heights), dims[dim] // shards_of).reshape((-1,) + (1,) * (len(dims) - 1 - dim))
    return level


def routed_block(rng, own, number, rows, count, top, bound, skew):
    order = jax.random.permutation(rng, count)
    heavy_load, common = portions_of(count, rows * top, bound, skew, True), portions_of(count, rows * top, bound, skew, False)
    places = jnp.arange(count)

    def named(tallies, offset_by):
        used = int((tallies > 0).sum())
        fixed = max(1, used // 4)
        moved = fixed + (places - fixed + offset_by * (used - fixed)) % max(1, count - fixed)
        return jnp.zeros((count,), jnp.int32).at[order[jnp.where(places < fixed, places, moved)]].set(jnp.asarray(tallies, jnp.int32))

    tallies = jnp.where(number % 4 == 0, named(heavy_load, number // 4), named(common, number - number // 4 - 1))
    mixed = jax.random.permutation(jax.random.fold_in(own, 3), count)
    source_of, sink = mixed[0:count // 2 * 2:2], mixed[1:count // 2 * 2:2]
    margin = jnp.minimum(tallies[source_of] - 1, bound - tallies[sink]) // 2
    margin = jnp.where((source_of == order[0]) | (sink == order[0]) | (tallies[sink] == 0), 0, jnp.maximum(margin, 0))
    moved = jax.random.randint(jax.random.fold_in(own, 4), (count // 2,), 0, 1 << 20) % (margin + 1)
    tallies = tallies.at[source_of].add(-moved).at[sink].add(moved)
    members = jnp.searchsorted(jnp.cumsum(tallies), jnp.arange(rows * top), side="right").astype(jnp.int32)
    grid = members.reshape(top, rows).T
    grid = grid[jax.random.permutation(jax.random.fold_in(own, 1), rows)]
    offset_by = jax.random.randint(jax.random.fold_in(own, 2), (rows, 1), 0, top)
    return jnp.take_along_axis(grid, (jnp.arange(top)[None, :] + offset_by) % top, axis=1)


def portions_of(amount, total, limit, slope, full):
    loads = [(1 << 20) // math.isqrt(rank ** slope) + 1 for rank in range(1, amount + 1)]
    largest = limit if full else min(limit, max(-(-total // amount), total * loads[0] // sum(loads)))
    least = 1 if total - largest >= amount - 1 else 0
    holding, rest = [largest] + [least] * (amount - 1), total - largest - least * (amount - 1)
    while rest > 0:
        movable = [i for i in range(1, amount) if holding[i] < largest] or [i for i in range(1, amount) if holding[i] < limit]
        pool, budget = sum([loads[i] for i in movable]), rest
        for i in movable:
            more = min(limit - holding[i], max(1, budget * loads[i] // pool), rest)
            holding[i] = holding[i] + more
            rest = rest - more
    return np.array(holding)


def normal_values(rng, dims, width, bound, pieces=(), held_as=jnp.bfloat16):
    entries = jax.random.normal(rng, dims, jnp.float32) * width
    if len(pieces) > 0:
        entries = shard_levels(rng, dims, pieces, -0.22, 0.18) * entries
    return jnp.clip(entries, min=-bound, max=bound).astype(held_as)


def setup_inputs(seed: int = 0) -> dict:
    keys = jax.random.split(jax.random.key(seed), 12)
    tokens = normal_values(keys[0], (TOKENS, D), 1.0, 6.0, ((0, 128),))
    routes_keys = jax.random.split(jax.random.fold_in(keys[1], 1), TOKENS // TOK_DEV)
    routes_turns = jax.random.permutation(jax.random.fold_in(keys[1], 3), TOKENS // TOK_DEV)
    routes = jax.vmap(lambda own, number: routed_block(jax.random.fold_in(keys[1], 2), own, number, TOK_DEV, EXPERTS, TOPK, CAP, 2))(routes_keys, routes_turns).reshape((TOKENS, TOPK))
    affinity = normal_values(keys[2], (TOKENS, TOPK), 2.0, 8.0, ((0, 128),), jnp.float32)
    w_gate = normal_values(keys[3], (EXPERTS, D, FF), D ** -0.5, 0.09375, ((0, 128),))
    w_up = normal_values(keys[4], (EXPERTS, D, FF), D ** -0.5, 0.09375, ((0, 128),))
    w_down = normal_values(keys[5], (EXPERTS, FF, D), FF ** -0.5, 0.1875, ((0, 128),))
    q_latent = normal_values(keys[6], (SEQS, HEADS, LAT), 1.0, 6.0, ((0, 128),))
    q_rope = draw_q_rope(jax.random.fold_in(keys[11], 71), 0)
    cache_latent = normal_values(keys[8], (SEQS, CACHE, LAT), 1.0, 6.0, ((0, 128),))
    cache_rope = draw_cache_rope(jax.random.fold_in(keys[11], 71), 0)
    lengths = draw_lengths(jax.random.fold_in(keys[11], 71), 0)
    return {"tokens": tokens, "routes": routes, "affinity": affinity, "w_gate": w_gate, "w_up": w_up, "w_down": w_down, "q_latent": q_latent, "q_rope": q_rope, "cache_latent": cache_latent, "cache_rope": cache_rope, "lengths": lengths}


qk_scale = 192.0 ** -0.5
route_scale = 2.5


def reference(tokens, routes, affinity, w_gate, w_up, w_down, q_latent, q_rope, cache_latent, cache_rope, lengths):
    devices = TOKENS // TOK_DEV
    pair_count = TOKENS * TOPK
    per_block = TOK_DEV * TOPK
    sig = jax.nn.sigmoid(affinity)
    weight = route_scale * sig / jnp.sum(sig, axis=1, keepdims=True)
    blocks = routes.reshape(devices, per_block).astype(jnp.int32)
    experts_row = jnp.arange(EXPERTS).astype(jnp.int32)
    onehot = (blocks[:, :, None] == experts_row[None, None, :]).astype(jnp.int32)
    ranks_run = jnp.cumsum(onehot, axis=1) - 1
    slot_of = jnp.sum(ranks_run * onehot, axis=2).astype(jnp.int32)
    source = jnp.arange(devices).astype(jnp.int32)[:, None]
    position = (source * CAP + slot_of).astype(jnp.int32)
    pair_ids = jnp.arange(pair_count).astype(jnp.int32).reshape(devices, per_block)
    table = jnp.full((EXPERTS, devices * CAP), pair_count, jnp.int32).at[blocks, position].set(pair_ids)
    tok_table = jnp.where(table < pair_count, table // TOPK, TOKENS).astype(jnp.int32)
    weight_pad = jnp.concatenate([weight.reshape(-1), jnp.zeros((1,), jnp.float32)])
    wt_table = weight_pad[table]
    padded = jnp.concatenate([tokens, jnp.zeros((1, D), jnp.bfloat16)], axis=0)

    def per_expert(total, items):
        toks, wts, gate_w, up_w, down_w = items
        rows = padded[toks]
        gate = jnp.dot(rows, gate_w, preferred_element_type=jnp.float32)
        upper = jnp.dot(rows, up_w, preferred_element_type=jnp.float32)
        hidden = (jax.nn.silu(gate) * upper).astype(jnp.bfloat16)
        result = jnp.dot(hidden, down_w, preferred_element_type=jnp.float32).astype(jnp.bfloat16)
        total = total.at[toks].add(wts[:, None] * result.astype(jnp.float32))
        return total, None

    start = jnp.zeros((TOKENS + 1, D), jnp.float32)
    total, unused = lax.scan(per_expert, start, (tok_table, wt_table, w_gate, w_up, w_down))
    moe_out = total[:TOKENS].astype(jnp.bfloat16)

    positions = jnp.arange(CACHE).astype(jnp.int32)

    def per_sequence(items):
        q_lat, q_rot, c_lat, c_rot, length = items
        q_rot = q_rot.reshape(HEADS, ROPE)
        scores = jnp.dot(q_lat, c_lat.T, preferred_element_type=jnp.float32)
        scores = scores + jnp.dot(q_rot, c_rot, preferred_element_type=jnp.float32)
        scores = scores * qk_scale
        valid = positions[None, :] < length
        scores = jnp.where(valid, scores, -1e30)
        top = jnp.max(scores, axis=1, keepdims=True)
        expo = jnp.where(valid, jnp.exp(scores - top), 0.0)
        probs = (expo / jnp.sum(expo, axis=1, keepdims=True)).astype(jnp.bfloat16)
        result = jnp.dot(probs, c_lat, preferred_element_type=jnp.float32).astype(jnp.bfloat16)
        return result.reshape(HEADS * LAT)

    attn_out = lax.map(per_sequence, (q_latent, q_rope, cache_latent, cache_rope, lengths))
    return moe_out, attn_out
```

```python
import functools

import jax
import jax.numpy as jnp
from jax import lax
from jax.experimental import pallas as pl
from jax.experimental.pallas import tpu as pltpu
from jax.sharding import PartitionSpec as P

MESH = pl.DeviceIdType.MESH
F32 = jnp.float32
BF16 = jnp.bfloat16

ROTATIONS = (("z", "x", "y"), ("x", "y", "z"), ("y", "z", "x"))
TILES = ((5, 5, 4), (4, 5, 5))
LANE = 128
SIDE = 4
TOK = 16
SLOTS = 2
LINE = 2 * SIDE
SOURCES = SIDE * SIDE
HELD = SOURCES * TOK
BLOCK = SOURCES * SLOTS
ROWS = LINE * BLOCK
qk_scale = 192.0 ** (-0.5)
route_scale = 2.5


def columns():
    table, start = [], 0
    for chunk in TILES:
        row = []
        for tiles in chunk:
            row.append((start * LANE, tiles * LANE))
            start += tiles
        table.append(row)
    return table


COLS = columns()
CHUNKS = len(TILES)
PARTS = [(c, r) for c in range(CHUNKS) for r in range(3)]


def dot(a, b):
    return jnp.dot(a, b, preferred_element_type=F32)


def dot_nt(a, b):
    return lax.dot_general(a, b, (((1,), (1,)), ((), ())), preferred_element_type=F32)


def rows_at(index, size):
    return pl.ds(pl.multiple_of(index * size, size), size)


def iota(shape, dim):
    return lax.broadcasted_iota(jnp.int32, shape, dim)


def order_of(rotation, digits):
    a, b, c = ROTATIONS[rotation]
    return (digits[c] * 2 + digits["core"]) * BLOCK + digits["slot"] * SOURCES + digits[b] * SIDE + digits[a]


def digits_of(rotation, index):
    a, b, c = ROTATIONS[rotation]
    return {
        c: index // (2 * BLOCK),
        "core": (index // BLOCK) % 2,
        "slot": (index // SOURCES) % SLOTS,
        b: (index // SIDE) % SIDE,
        a: index % SIDE,
    }


def kernel(
    tokens, routes, affinity, w_gate, w_up, w_down, q_latent, q_rope, cache_latent, cache_rope, lengths,
    moe_out, attn_out,
    *scratch,
):
    it = iter(scratch)

    def take():
        return [[next(it) for _ in range(3)] for _ in range(CHUNKS)]

    held, send, recv, back, part, sum_b, sum_a = (take() for _ in range(7))
    aligned, gate_acc, up_acc, hidden, hidden_r, weigh, perm = (next(it) for _ in range(7))
    routes_v, affinity_v, gate_v, up_v, down_v = (next(it) for _ in range(5))
    ql_v, qr_v, cl_v, cr_v, len_s, q_heads, att, attn_v, moe_v = (next(it) for _ in range(9))
    send_sem, recv_sem, local_sem, weight_sem = (next(it) for _ in range(4))

    group, member = lax.axis_index("group"), lax.axis_index("member")
    me = {"z": group // 2, "core": group % 2, "x": member // 4, "y": member % 4}

    def device(**other):
        at = dict(me)
        at.update(other)
        return (at["z"] * 2 + at["core"], at["x"] * 4 + at["y"])

    barrier = pltpu.get_barrier_semaphore()
    other_core = 1 - me["core"]
    pl.semaphore_signal(barrier, inc=1, device_id=device(core=other_core), device_id_type=MESH)
    for axis in "zxy":
        for k in (1, 3, 2):
            place = (me[axis] + k) % SIDE
            for core in (me["core"], other_core):
                pl.semaphore_signal(barrier, inc=1, device_id=device(**{axis: place, "core": core}), device_id_type=MESH)

    def own_slot(r):
        a, b, _ = ROTATIONS[r]
        return rows_at(me[b] * SIDE + me[a], TOK)

    local = []

    def bring(src, dst):
        copy = pltpu.make_async_copy(src, dst, local_sem.at[len(local)])
        copy.start()
        local.append(copy)
        return copy

    small = [bring(routes, routes_v), bring(affinity, affinity_v)]
    token_copies = []
    for c, r in PARTS:
        start, width = COLS[c][r]
        token_copies.append(bring(tokens.at[:, pl.ds(start, width)], held[c][r].at[own_slot(r), pl.ds(0, width)]))
    attention_copies = [bring(q_rope, qr_v), bring(q_latent, ql_v), bring(cache_latent, cl_v), bring(cache_rope, cr_v), bring(lengths, len_s)]
    weight_copies = {}
    half = gate_v.shape[0] // CHUNKS
    number = 0
    for c in range(CHUNKS):
        for name, src, dst in (("gate", w_gate, gate_v), ("up", w_up, up_v)):
            copy = pltpu.make_async_copy(src.at[0, pl.ds(c * half, half)], dst.at[pl.ds(c * half, half)], weight_sem.at[number])
            copy.start()
            weight_copies[name, c] = copy
            number += 1
    down_copy = pltpu.make_async_copy(w_down.at[0], down_v, weight_sem.at[number])
    down_copy.start()

    for copy in small:
        copy.wait()
    sig = 1.0 / (1.0 + jnp.exp(-affinity_v[...]))
    weight = route_scale * sig / jnp.sum(sig, axis=1, keepdims=True)
    chosen = routes_v[...]
    lanes = iota((TOK, LANE), 1)
    dense = jnp.zeros((TOK, LANE), F32)
    hit = jnp.zeros((TOK, LANE), F32)
    for j in range(chosen.shape[1]):
        same = chosen[:, j : j + 1] == lanes
        dense = jnp.where(same, weight[:, j : j + 1], dense)
        hit = jnp.where(same, 1.0, hit)
    before = (iota((TOK, TOK), 1) < iota((TOK, TOK), 0)).astype(F32).astype(BF16)
    rank = dot(before, hit.astype(BF16))
    code = jnp.where(rank > 0.5, -dense, dense).astype(BF16)
    for r in range(3):
        held[0][r][own_slot(r), pl.ds(COLS[0][r][1], LANE)] = code

    def remote(src, dst, stage, c, r, to):
        return pltpu.make_async_remote_copy(
            src_ref=src, dst_ref=dst,
            send_sem=send_sem.at[stage, c * 3 + r], recv_sem=recv_sem.at[stage, c * 3 + r],
            device_id=to, device_id_type=MESH,
        )

    def await_bytes(ref, sem, stage, c, r):
        pltpu.make_async_copy(ref, ref, sem.at[stage, c * 3 + r]).wait()

    for copy in token_copies:
        copy.wait()
    pl.semaphore_wait(barrier, 1 + 3 * 3 * 2)

    for c, r in PARTS:
        a = ROTATIONS[r][0]
        block = held[c][r].at[own_slot(r)]
        for k in (1, 3, 2):
            remote(block, block, 0, c, r, device(**{a: (me[a] + k) % SIDE})).start()

    for r in (1, 2):
        here = order_of(r, digits_of(0, iota((ROWS, ROWS), 0)))
        perm[r - 1] = jnp.where(here == iota((ROWS, ROWS), 1), 1.0, 0.0).astype(BF16)

    for c, r in PARTS:
        b = ROTATIONS[r][1]
        await_bytes(held[c][r].at[pl.ds(0, 3 * TOK)], recv_sem, 0, c, r)
        block = held[c][r].at[rows_at(me[b], SIDE * TOK)]
        for k in (1, 3, 2):
            remote(block, block, 1, c, r, device(**{b: (me[b] + k) % SIDE})).start()

    for copy in attention_copies:
        copy.wait()
    seqs, heads, latent = ql_v.shape
    rope = cr_v.shape[1]
    cached = cr_v.shape[2]

    def split_heads(p, _):
        pair = qr_v[:, pl.ds(pl.multiple_of(p * LANE, LANE), LANE)].astype(F32)
        q_heads[pl.ds(2 * p, seqs, stride=heads), :] = pair
        q_heads[pl.ds(2 * p + 1, seqs, stride=heads), :] = pltpu.roll(pair, LANE - rope, 1)
        return 0

    lax.fori_loop(0, heads // 2, split_heads, 0)

    def attend(s, _):
        q_rot = q_heads[rows_at(s, heads), :][:, :rope].astype(BF16)
        keys = cl_v[s]
        scores = (dot_nt(ql_v[s], keys) + dot(q_rot, cr_v[s])) * qk_scale
        valid = iota((heads, cached), 1) < len_s[s]
        scores = jnp.where(valid, scores, -1e30)
        top = jnp.max(scores, axis=1, keepdims=True)
        expo = jnp.where(valid, jnp.exp(scores - top), 0.0)
        probs = (expo / jnp.sum(expo, axis=1, keepdims=True)).astype(BF16)
        mixed = dot(probs, keys)
        for q in range(latent // LANE):
            att[q, rows_at(s, heads), :] = mixed[:, q * LANE : (q + 1) * LANE]
        return 0

    lax.fori_loop(0, seqs, attend, 0)

    def join_heads(h, _):
        for q in range(latent // LANE):
            lane = pl.ds(pl.multiple_of(h * latent + q * LANE, LANE), LANE)
            attn_v[:, lane] = att[q, pl.ds(h, seqs, stride=heads), :].astype(BF16)
        return 0

    lax.fori_loop(0, heads, join_heads, 0)
    attn_copy = pltpu.make_async_copy(attn_v, attn_out, local_sem.at[len(local)])
    attn_copy.start()

    source_row = iota((BLOCK, HELD), 0)
    own_source = (source_row % SOURCES) == (iota((BLOCK, HELD), 1) // TOK)
    slot_sign = jnp.where(source_row < SOURCES, 1.0, -1.0)
    line_order = ((1, 0), (3, 1), (2, 0), (3, 0), (1, 1), (2, 1), (0, 1))

    def own_block(r):
        return rows_at(me[ROTATIONS[r][2]] * 2 + me["core"], BLOCK)

    def line_peer(r, k, flip):
        c_axis = ROTATIONS[r][2]
        place, core = (me[c_axis] + k) % SIDE, (me["core"] + flip) % 2
        return rows_at(place * 2 + core, BLOCK), device(**{c_axis: place, "core": core})

    pick = [None] * 3
    for c, r in PARTS:
        width = COLS[c][r][1]
        await_bytes(held[c][r].at[pl.ds(0, 3 * SIDE * TOK)], recv_sem, 1, c, r)
        if c == 0:
            c_axis = ROTATIONS[r][2]
            peer = iota((LINE, LANE), 0)
            at = dict(me)
            at[c_axis] = peer // 2
            expert = (at["z"] * 2 + peer % 2) * 16 + at["x"] * 4 + at["y"]
            select = jnp.where(expert == iota((LINE, LANE), 1), 1.0, 0.0).astype(BF16)
            codes = dot_nt(select, held[c][r][:, pl.ds(width, LANE)])
            ones, scaled = [], []
            for e in range(LINE):
                signed = codes[e : e + 1, :] * slot_sign
                good = jnp.logical_and(own_source, signed > 0.0)
                ones.append(jnp.where(good, 1.0, 0.0).astype(BF16))
                scaled.append(jnp.where(good, signed, 0.0))
            pick[r] = jnp.concatenate(ones, axis=0)
            weigh[r] = jnp.concatenate(scaled, axis=0).T.astype(BF16)
        send[c][r][...] = dot(pick[r], held[c][r][:, pl.ds(0, width)]).astype(BF16)
        for k, flip in line_order:
            block, to = line_peer(r, k, flip)
            remote(send[c][r].at[block], recv[c][r].at[own_block(r)], 2, c, r, to).start()
        recv[c][r][own_block(r), :] = send[c][r][own_block(r), :]

    ff = gate_v.shape[1]
    step = 256
    for c in range(CHUNKS):
        weight_copies["gate", c].wait()
        weight_copies["up", c].wait()
        for r in range(3):
            start, width = COLS[c][r]
            await_bytes(recv[c][r].at[pl.ds(0, (LINE - 1) * BLOCK)], recv_sem, 2, c, r)
            inside = pl.ds(start - c * half, width)
            if r == 0:
                aligned[:, inside] = recv[c][r][...]
            else:
                aligned[:, inside] = dot(perm[r - 1], recv[c][r][...]).astype(BF16)

        def ff_tile(n, _, c=c):
            tile = pl.ds(pl.multiple_of(n * step, step), step)
            gate = dot(aligned[...], gate_v[pl.ds(c * half, half), tile])
            upper = dot(aligned[...], up_v[pl.ds(c * half, half), tile])
            if c > 0:
                gate = gate + gate_acc[:, tile]
                upper = upper + up_acc[:, tile]
            if c < CHUNKS - 1:
                gate_acc[:, tile] = gate
                up_acc[:, tile] = upper
            else:
                hidden[:, tile] = (gate / (1.0 + jnp.exp(-gate)) * upper).astype(BF16)
            return 0

        lax.fori_loop(0, ff // step, ff_tile, 0)

    for r in (1, 2):
        hidden_r[r - 1] = lax.dot_general(
            perm[r - 1], hidden[...], (((0,), (0,)), ((), ())), preferred_element_type=F32
        ).astype(BF16)
    down_copy.wait()
    for c, r in PARTS:
        start, width = COLS[c][r]
        rows = hidden[...] if r == 0 else hidden_r[r - 1]
        await_bytes(recv[c][r].at[pl.ds(0, (LINE - 1) * BLOCK)], send_sem, 2, c, r)
        send[c][r][...] = dot(rows, down_v[:, pl.ds(start, width)]).astype(BF16)
        for k, flip in line_order:
            block, to = line_peer(r, k, flip)
            remote(send[c][r].at[block], back[c][r].at[own_block(r)], 3, c, r, to).start()
        back[c][r][own_block(r), :] = send[c][r][own_block(r), :]

    for c, r in PARTS:
        b = ROTATIONS[r][1]
        await_bytes(back[c][r].at[pl.ds(0, (LINE - 1) * BLOCK)], recv_sem, 3, c, r)
        part[c][r][...] = dot(weigh[r], back[c][r][...]).astype(BF16)
        own = rows_at(me[b], SIDE * TOK)
        for k in (1, 3, 2):
            place = (me[b] + k) % SIDE
            remote(part[c][r].at[rows_at(place, SIDE * TOK)], sum_b[c][r].at[own], 4, c, r, device(**{b: place})).start()
        sum_b[c][r][own, :] = part[c][r][own, :]
    for c, r in PARTS:
        a, b, _ = ROTATIONS[r]
        size = SIDE * TOK
        await_bytes(sum_b[c][r].at[pl.ds(0, 3 * size)], recv_sem, 4, c, r)
        total = sum_b[c][r][pl.ds(0, size), :].astype(F32)
        for k in range(1, SIDE):
            total = total + sum_b[c][r][pl.ds(k * size, size), :].astype(F32)
        await_bytes(part[c][r].at[pl.ds(0, 3 * size)], send_sem, 4, c, r)
        part[c][r][pl.ds(0, size), :] = total.astype(BF16)
        own = rows_at(me[a], TOK)
        for k in (1, 3, 2):
            place = (me[a] + k) % SIDE
            remote(part[c][r].at[rows_at(place, TOK)], sum_a[c][r].at[own], 5, c, r, device(**{a: place})).start()
        sum_a[c][r][own, :] = part[c][r][own, :]
    for c, r in PARTS:
        start, width = COLS[c][r]
        await_bytes(sum_a[c][r].at[pl.ds(0, 3 * TOK)], recv_sem, 5, c, r)
        total = sum_a[c][r][pl.ds(0, TOK), :].astype(F32)
        for k in range(1, SIDE):
            total = total + sum_a[c][r][pl.ds(k * TOK, TOK), :].astype(F32)
        moe_v[:, pl.ds(start, width)] = total.astype(BF16)
    moe_copy = pltpu.make_async_copy(moe_v, moe_out, local_sem.at[len(local) + 1])
    moe_copy.start()

    for c, r in PARTS:
        await_bytes(held[c][r].at[pl.ds(0, 3 * TOK)], send_sem, 0, c, r)
        await_bytes(held[c][r].at[pl.ds(0, 3 * SIDE * TOK)], send_sem, 1, c, r)
        await_bytes(recv[c][r].at[pl.ds(0, (LINE - 1) * BLOCK)], send_sem, 3, c, r)
        await_bytes(sum_a[c][r].at[pl.ds(0, 3 * TOK)], send_sem, 5, c, r)
    attn_copy.wait()
    moe_copy.wait()


def per_device(tokens, routes, affinity, w_gate, w_up, w_down, q_latent, q_rope, cache_latent, cache_rope, lengths):
    tok_dev, width = tokens.shape
    ff = w_gate.shape[2]
    seqs, heads, latent = q_latent.shape
    half = width // CHUNKS

    def buffers(rows, extra=0):
        return [
            pltpu.VMEM((rows, COLS[c][r][1] + (extra if c == 0 else 0)), BF16) for c, r in PARTS
        ]

    scratch = (
        buffers(HELD, LANE)
        + buffers(ROWS) * 3
        + buffers(HELD) * 2
        + buffers(SIDE * TOK)
        + [
            pltpu.VMEM((ROWS, half), BF16),
            pltpu.VMEM((ROWS, ff), F32),
            pltpu.VMEM((ROWS, ff), F32),
            pltpu.VMEM((ROWS, ff), BF16),
            pltpu.VMEM((2, ROWS, ff), BF16),
            pltpu.VMEM((3, HELD, ROWS), BF16),
            pltpu.VMEM((2, ROWS, ROWS), BF16),
            pltpu.VMEM(routes.shape, jnp.int32),
            pltpu.VMEM(affinity.shape, F32),
            pltpu.VMEM((width, ff), BF16),
            pltpu.VMEM((width, ff), BF16),
            pltpu.VMEM((ff, width), BF16),
            pltpu.VMEM(q_latent.shape, BF16),
            pltpu.VMEM(q_rope.shape, BF16),
            pltpu.VMEM(cache_latent.shape, BF16),
            pltpu.VMEM(cache_rope.shape, BF16),
            pltpu.SMEM(lengths.shape, jnp.int32),
            pltpu.VMEM((seqs * heads, LANE), F32),
            pltpu.VMEM((latent // LANE, seqs * heads, LANE), F32),
            pltpu.VMEM((seqs, heads * latent), BF16),
            pltpu.VMEM((tok_dev, width), BF16),
            pltpu.SemaphoreType.DMA((6, len(PARTS))),
            pltpu.SemaphoreType.DMA((6, len(PARTS))),
            pltpu.SemaphoreType.DMA((2 + len(PARTS) + 5 + 2,)),
            pltpu.SemaphoreType.DMA((2 * CHUNKS + 1,)),
        ]
    )
    return pl.pallas_call(
        kernel,
        out_shape=(
            jax.ShapeDtypeStruct((tok_dev, width), BF16),
            jax.ShapeDtypeStruct((seqs, heads * latent), BF16),
        ),
        in_specs=[pl.BlockSpec(memory_space=pl.ANY)] * 11,
        out_specs=[pl.BlockSpec(memory_space=pl.ANY)] * 2,
        scratch_shapes=scratch,
        compiler_params=pltpu.CompilerParams(
            collective_id=0, has_side_effects=True, vmem_limit_bytes=62 * 1024 * 1024
        ),
    )(tokens, routes, affinity, w_gate, w_up, w_down, q_latent, q_rope, cache_latent, cache_rope, lengths)


def solution(mesh):
    rows = P(("group", "member"), None)
    cube = P(("group", "member"), None, None)
    return jax.shard_map(
        per_device,
        mesh=mesh,
        in_specs=(rows, rows, rows, cube, cube, cube, cube, rows, cube, cube, P(("group", "member"))),
        out_specs=(rows, rows),
        check_vma=False,
    )
```

```python
import functools

import jax
import jax.numpy as jnp
from jax import lax
from jax.experimental import pallas as pl
from jax.experimental.pallas import tpu as pltpu
from jax.sharding import PartitionSpec as P

MESH = pl.DeviceIdType.MESH
F32 = jnp.float32
BF16 = jnp.bfloat16

ROTATIONS = (("z", "x", "y"), ("x", "y", "z"), ("y", "z", "x"))
TILES = ((9, 10, 9),)
LANE = 128
SIDE = 4
TOK = 16
SLOTS = 2
LINE = 2 * SIDE
SOURCES = SIDE * SIDE
WAVES = 2
FEW = SOURCES // WAVES
HELD = FEW * TOK
BLOCK = FEW * SLOTS
ROWS = LINE * BLOCK
GATHER_A, GATHER_B, TO_EXPERT, FROM_EXPERT, SUM_B, SUM_A = range(6)
STAGES = 6
ATTEND = (4, 4)
qk_scale = 192.0 ** (-0.5)
route_scale = 2.5


def columns():
    table, start = [], 0
    for chunk in TILES:
        row = []
        for tiles in chunk:
            row.append((start * LANE, tiles * LANE))
            start += tiles
        table.append(row)
    return table


COLS = columns()
CHUNKS = len(TILES)
PARTS = [(c, r) for c in range(CHUNKS) for r in range(3)]


def dot(a, b):
    return jnp.dot(a, b, preferred_element_type=F32)


def dot_nt(a, b):
    return lax.dot_general(a, b, (((1,), (1,)), ((), ())), preferred_element_type=F32)


def rows_at(index, size):
    return pl.ds(pl.multiple_of(index * size, size), size)


def iota(shape, dim):
    return lax.broadcasted_iota(jnp.int32, shape, dim)


def order_of(rotation, digits):
    a, b, c = ROTATIONS[rotation]
    place = digits[b] * (SIDE // 2) + digits[a] // 2
    return (digits[c] * 2 + digits["core"]) * BLOCK + digits["slot"] * FEW + place


def digits_of(rotation, wave, index):
    a, b, c = ROTATIONS[rotation]
    found = {
        c: index // (2 * BLOCK),
        "core": (index // BLOCK) % 2,
        "slot": (index // FEW) % SLOTS,
        b: (index // 2) % SIDE,
    }
    found[a] = 2 * (index % 2) + (found[b] + found[c] + wave) % 2
    return found


def kernel(
    tokens, routes, affinity, w_gate, w_up, w_down, q_latent, q_rope, cache_latent, cache_rope, lengths,
    moe_out, attn_out,
    *scratch,
):
    it = iter(scratch)

    def take():
        return [[next(it) for _ in range(3)] for _ in range(CHUNKS)]

    held = take()
    send, recv, back, part, sum_b = ([take() for _ in range(WAVES)] for _ in range(5))
    sum_a = take()
    aligned, hidden, hidden_r, weigh, perm = (next(it) for _ in range(5))
    routes_v, affinity_v, gate_v, up_v, down_v = (next(it) for _ in range(5))
    ql_v, qr_v, cl_v, cr_v, len_s, q_heads, att, attn_v, moe_v = (next(it) for _ in range(9))
    send_sem, recv_sem, local_sem, weight_sem = (next(it) for _ in range(4))

    group, member = lax.axis_index("group"), lax.axis_index("member")
    me = {"z": group // 2, "core": group % 2, "x": member // 4, "y": member % 4}

    def device(**other):
        at = dict(me)
        at.update(other)
        return (at["z"] * 2 + at["core"], at["x"] * 4 + at["y"])

    barrier = pltpu.get_barrier_semaphore()
    other_core = 1 - me["core"]
    pl.semaphore_signal(barrier, inc=1, device_id=device(core=other_core), device_id_type=MESH)
    for axis in "zxy":
        for k in (1, 3, 2):
            place = (me[axis] + k) % SIDE
            for core in (me["core"], other_core):
                pl.semaphore_signal(barrier, inc=1, device_id=device(**{axis: place, "core": core}), device_id_type=MESH)

    parity = (me["x"] + me["y"] + me["z"]) % 2

    def slot_of(r, a_place):
        return rows_at(me[ROTATIONS[r][1]] * 2 + a_place // 2, TOK)

    def own_slot(r):
        return slot_of(r, me[ROTATIONS[r][0]])

    local = []

    def bring(src, dst):
        copy = pltpu.make_async_copy(src, dst, local_sem.at[len(local)])
        copy.start()
        local.append(copy)
        return copy

    small = [bring(routes, routes_v), bring(affinity, affinity_v)]
    token_copies = []
    for c, r in PARTS:
        start, width = COLS[c][r]
        token_copies.append(bring(tokens.at[:, pl.ds(start, width)], held[c][r].at[parity, own_slot(r), pl.ds(0, width)]))
    attention_copies = [bring(q_rope, qr_v), bring(q_latent, ql_v), bring(cache_latent, cl_v), bring(cache_rope, cr_v), bring(lengths, len_s)]
    weight_copies = []
    for number, (src, dst) in enumerate(((w_gate, gate_v), (w_up, up_v), (w_down, down_v))):
        weight_copies.append(pltpu.make_async_copy(src.at[0], dst, weight_sem.at[number]))

    for copy in small:
        copy.wait()
    sig = 1.0 / (1.0 + jnp.exp(-affinity_v[...]))
    weight = route_scale * sig / jnp.sum(sig, axis=0, keepdims=True)
    chosen = routes_v[...]
    expert_row = iota((LANE, TOK), 0)
    dense = jnp.zeros((LANE, TOK), F32)
    hit = jnp.zeros((LANE, TOK), F32)
    for j in range(chosen.shape[0]):
        same = chosen[j : j + 1, :] == expert_row
        dense = jnp.where(same, weight[j : j + 1, :], dense)
        hit = jnp.where(same, 1.0, hit)
    before = jnp.where(iota((TOK, TOK), 0) < iota((TOK, TOK), 1), 1.0, 0.0).astype(BF16)
    rank = dot(hit.astype(BF16), before)
    signed = jnp.where(rank > 0.5, -dense, dense)
    code = jnp.concatenate([signed, jnp.zeros((LANE, LANE - TOK), F32)], axis=1).T[:TOK].astype(BF16)
    for r in range(3):
        held[0][r][parity, own_slot(r), pl.ds(COLS[0][r][1], LANE)] = code

    def remote(src, dst, stage, wave, c, r, to):
        part_of = c * 3 + r
        return pltpu.make_async_remote_copy(
            src_ref=src, dst_ref=dst,
            send_sem=send_sem.at[stage, wave, part_of], recv_sem=recv_sem.at[stage, wave, part_of],
            device_id=to, device_id_type=MESH,
        )

    def await_rows(ref, rows, sem, stage, wave, c, r):
        some = ref.at[pl.ds(0, rows)]
        pltpu.make_async_copy(some, some, sem.at[stage, wave, c * 3 + r]).wait()

    for copy in token_copies:
        copy.wait()
    seqs, heads, latent = ql_v.shape
    rope = cr_v.shape[1]
    cached = cr_v.shape[2]

    def split_heads(p, _):
        pair = qr_v[:, pl.ds(pl.multiple_of(p * LANE, LANE), LANE)].astype(F32)
        q_heads[pl.ds(2 * p, seqs, stride=heads), :] = pair
        q_heads[pl.ds(2 * p + 1, seqs, stride=heads), :] = pltpu.roll(pair, LANE - rope, 1)
        return 0

    def attend(s, _):
        q_rot = q_heads[rows_at(s, heads), :][:, :rope].astype(BF16)
        keys = cl_v[s]
        scores = (dot_nt(ql_v[s], keys) + dot(q_rot, cr_v[s])) * qk_scale
        valid = iota((heads, cached), 1) < len_s[s]
        scores = jnp.where(valid, scores, -1e30)
        top = jnp.max(scores, axis=1, keepdims=True)
        expo = jnp.where(valid, jnp.exp(scores - top), 0.0)
        probs = (expo / jnp.sum(expo, axis=1, keepdims=True)).astype(BF16)
        mixed = dot(probs, keys)
        for q in range(latent // LANE):
            att[q, rows_at(s, heads), :] = mixed[:, q * LANE : (q + 1) * LANE]
        return 0

    def join_heads(h, _):
        for q in range(latent // LANE):
            lane = pl.ds(pl.multiple_of(h * latent + q * LANE, LANE), LANE)
            attn_v[:, lane] = att[q, pl.ds(h, seqs, stride=heads), :].astype(BF16)
        return 0

    pl.semaphore_wait(barrier, 1 + 3 * 3 * 2)

    for stage, axis in ((GATHER_A, 0), (GATHER_B, 1)):
        for c, r in PARTS:
            along = ROTATIONS[r][axis]
            block = held[c][r].at[parity, own_slot(r)]
            for k in (1, 3, 2):
                remote(block, block, stage, parity, c, r, device(**{along: (me[along] + k) % SIDE})).start()

    for copy in attention_copies:
        copy.wait()
    for copy in weight_copies:
        copy.start()

    for wave in range(WAVES):
        for r in (1, 2):
            here = order_of(r, digits_of(0, wave, iota((ROWS, ROWS), 0)))
            perm[wave, r - 1] = jnp.where(here == iota((ROWS, ROWS), 1), 1.0, 0.0).astype(BF16)

    lax.fori_loop(0, heads // 2, split_heads, 0, unroll=8)
    lax.fori_loop(0, ATTEND[0], attend, 0, unroll=4)

    for wave in range(WAVES):
        for c, r in PARTS:
            a, b, _ = ROTATIONS[r]
            mine = held[c][r].at[wave]
            far = mine.at[slot_of(r, (me[a] + 2) % SIDE)]
            both = mine.at[rows_at(me[b], 2 * TOK)]

            @pl.when(parity == wave)
            def _():
                await_rows(mine, TOK, recv_sem, GATHER_A, wave, c, r)
                for k in (1, 3, 2):
                    remote(far, far, GATHER_B, wave, c, r, device(**{b: (me[b] + k) % SIDE})).start()

            @pl.when(parity != wave)
            def _():
                await_rows(mine, 2 * TOK, recv_sem, GATHER_A, wave, c, r)
                for k in (1, 3, 2):
                    remote(both, both, GATHER_B, wave, c, r, device(**{b: (me[b] + k) % SIDE})).start()

        if wave == 0:
            lax.fori_loop(ATTEND[0], seqs, attend, 0, unroll=ATTEND[1])
            lax.fori_loop(0, heads, join_heads, 0, unroll=8)
            attn_copy = pltpu.make_async_copy(attn_v, attn_out, local_sem.at[len(local)])
            attn_copy.start()

    place = iota((BLOCK, HELD), 0)
    own_source = place % FEW == iota((BLOCK, HELD), 1) // TOK
    slot_sign = jnp.where(place < FEW, 1.0, -1.0)
    line_order = ((1, 0), (3, 1), (2, 0), (3, 0), (1, 1), (2, 1), (0, 1))

    def own_block(r):
        return rows_at(me[ROTATIONS[r][2]] * 2 + me["core"], BLOCK)

    def line_peer(r, k, flip):
        c_axis = ROTATIONS[r][2]
        at, core = (me[c_axis] + k) % SIDE, (me["core"] + flip) % 2
        return rows_at(at * 2 + core, BLOCK), device(**{c_axis: at, "core": core})

    def exchange(outgoing, incoming, stage, wave, c, r):
        for k, flip in line_order:
            block, to = line_peer(r, k, flip)
            remote(outgoing.at[block], incoming.at[own_block(r)], stage, wave, c, r, to).start()
        incoming[own_block(r), :] = outgoing[own_block(r), :]

    for wave in range(WAVES):
        pick = {}
        for c, r in PARTS:
            width = COLS[c][r][1]
            await_rows(held[c][r].at[wave], 6 * TOK, recv_sem, GATHER_B, wave, c, r)
            if c == 0:
                c_axis = ROTATIONS[r][2]
                peer = iota((LINE, LANE), 0)
                at = dict(me)
                at[c_axis] = peer // 2
                expert = (at["z"] * 2 + peer % 2) * 16 + at["x"] * 4 + at["y"]
                select = jnp.where(expert == iota((LINE, LANE), 1), 1.0, 0.0).astype(BF16)
                codes = dot_nt(select, held[c][r][wave, :, pl.ds(width, LANE)])
                ones, scaled = [], []
                for e in range(LINE):
                    signed = codes[e : e + 1, :] * slot_sign
                    good = jnp.logical_and(own_source, signed > 0.0)
                    ones.append(jnp.where(good, 1.0, 0.0).astype(BF16))
                    scaled.append(jnp.where(good, signed, 0.0))
                pick[r] = jnp.concatenate(ones, axis=0)
                weigh[wave, r] = jnp.concatenate(scaled, axis=0).T.astype(BF16)
            send[wave][c][r][...] = dot(pick[r], held[c][r][wave, :, pl.ds(0, width)]).astype(BF16)
            exchange(send[wave][c][r], recv[wave][c][r], TO_EXPERT, wave, c, r)

    ff = gate_v.shape[1]
    step = 512
    for wave in range(WAVES):
        for c, r in PARTS:
            start, width = COLS[c][r]
            await_rows(recv[wave][c][r], ROWS - BLOCK, recv_sem, TO_EXPERT, wave, c, r)
            if r == 0:
                aligned[:, pl.ds(start, width)] = recv[wave][c][r][...]
            else:
                aligned[:, pl.ds(start, width)] = dot(perm[wave, r - 1], recv[wave][c][r][...]).astype(BF16)
        if wave == 0:
            for copy in weight_copies:
                copy.wait()

        def ff_tile(n, _):
            tile = pl.ds(pl.multiple_of(n * step, step), step)
            gate = dot(aligned[...], gate_v[:, tile])
            upper = dot(aligned[...], up_v[:, tile])
            hidden[:, tile] = (gate / (1.0 + jnp.exp(-gate)) * upper).astype(BF16)
            return 0

        lax.fori_loop(0, ff // step, ff_tile, 0, unroll=True)
        for r in (1, 2):
            hidden_r[r - 1] = lax.dot_general(
                perm[wave, r - 1], hidden[...], (((0,), (0,)), ((), ())), preferred_element_type=F32
            ).astype(BF16)
        for c, r in PARTS:
            start, width = COLS[c][r]
            rows = hidden[...] if r == 0 else hidden_r[r - 1]
            await_rows(send[wave][c][r], ROWS - BLOCK, send_sem, TO_EXPERT, wave, c, r)
            send[wave][c][r][...] = dot(rows, down_v[:, pl.ds(start, width)]).astype(BF16)
            exchange(send[wave][c][r], back[wave][c][r], FROM_EXPERT, wave, c, r)

    pair = 2 * TOK
    for wave in range(WAVES):
        for c, r in PARTS:
            b = ROTATIONS[r][1]
            await_rows(back[wave][c][r], ROWS - BLOCK, recv_sem, FROM_EXPERT, wave, c, r)
            mine = part[wave][c][r]
            mine[...] = dot(weigh[wave, r], back[wave][c][r][...]).astype(BF16)
            own = rows_at(me[b], pair)
            for k in (1, 3, 2):
                to = (me[b] + k) % SIDE
                remote(mine.at[rows_at(to, pair)], sum_b[wave][c][r].at[own], SUM_B, wave, c, r, device(**{b: to})).start()
            sum_b[wave][c][r][own, :] = mine[own, :]
    for wave in range(WAVES):
        for c, r in PARTS:
            a, b, _ = ROTATIONS[r]
            arrived = sum_b[wave][c][r]
            await_rows(arrived, 3 * pair, recv_sem, SUM_B, wave, c, r)
            total = arrived[pl.ds(0, pair), :].astype(F32)
            for k in range(1, SIDE):
                total = total + arrived[pl.ds(k * pair, pair), :].astype(F32)
            mine = part[wave][c][r]
            await_rows(mine, 3 * pair, send_sem, SUM_B, wave, c, r)
            mine[pl.ds(0, pair), :] = total.astype(BF16)
            own = rows_at(me[a], TOK)

            def give(to, c=c, r=r, wave=wave, mine=mine, own=own, a=a):
                remote(mine.at[rows_at(to // 2, TOK)], sum_a[c][r].at[own], SUM_A, wave, c, r, device(**{a: to})).start()

            @pl.when(parity == wave)
            def _():
                give((me[a] + 2) % SIDE)
                sum_a[c][r][own, :] = mine[rows_at(me[a] // 2, TOK), :]

            @pl.when(parity != wave)
            def _():
                give((me[a] + 1) % SIDE)
                give((me[a] + 3) % SIDE)

    for c, r in PARTS:
        start, width = COLS[c][r]
        await_rows(sum_a[c][r], 3 * TOK, recv_sem, SUM_A, parity, c, r)
        total = sum_a[c][r][pl.ds(0, TOK), :].astype(F32)
        for k in range(1, SIDE):
            total = total + sum_a[c][r][pl.ds(k * TOK, TOK), :].astype(F32)
        moe_v[:, pl.ds(start, width)] = total.astype(BF16)
    moe_copy = pltpu.make_async_copy(moe_v, moe_out, local_sem.at[len(local) + 1])
    moe_copy.start()

    for c, r in PARTS:
        await_rows(held[c][r].at[0], 3 * TOK, send_sem, GATHER_A, parity, c, r)
        for wave in range(WAVES):
            await_rows(back[wave][c][r], ROWS - BLOCK, send_sem, FROM_EXPERT, wave, c, r)
            await_rows(held[c][r].at[wave], 6 * TOK, send_sem, GATHER_B, wave, c, r)

            @pl.when(parity == wave)
            def _():
                await_rows(sum_a[c][r], TOK, send_sem, SUM_A, wave, c, r)

            @pl.when(parity != wave)
            def _():
                await_rows(sum_a[c][r], 2 * TOK, send_sem, SUM_A, wave, c, r)

    attn_copy.wait()
    moe_copy.wait()


def per_device(tokens, routes, affinity, w_gate, w_up, w_down, q_latent, q_rope, cache_latent, cache_rope, lengths):
    tok_dev, width = tokens.shape
    ff = w_gate.shape[2]
    seqs, heads, latent = q_latent.shape

    def buffers(rows):
        return [pltpu.VMEM((rows, COLS[c][r][1]), BF16) for c, r in PARTS]

    scratch = (
        [pltpu.VMEM((WAVES, HELD, COLS[c][r][1] + (LANE if c == 0 else 0)), BF16) for c, r in PARTS]
        + buffers(ROWS) * (3 * WAVES)
        + buffers(HELD) * (2 * WAVES)
        + buffers(SIDE * TOK)
        + [
            pltpu.VMEM((ROWS, width), BF16),
            pltpu.VMEM((ROWS, ff), BF16),
            pltpu.VMEM((2, ROWS, ff), BF16),
            pltpu.VMEM((WAVES, 3, HELD, ROWS), BF16),
            pltpu.VMEM((WAVES, 2, ROWS, ROWS), BF16),
            pltpu.VMEM(routes.shape[::-1], jnp.int32),
            pltpu.VMEM(affinity.shape[::-1], F32),
            pltpu.VMEM((width, ff), BF16),
            pltpu.VMEM((width, ff), BF16),
            pltpu.VMEM((ff, width), BF16),
            pltpu.VMEM(q_latent.shape, BF16),
            pltpu.VMEM(q_rope.shape, BF16),
            pltpu.VMEM(cache_latent.shape, BF16),
            pltpu.VMEM(cache_rope.shape, BF16),
            pltpu.SMEM(lengths.shape, jnp.int32),
            pltpu.VMEM((seqs * heads, LANE), F32),
            pltpu.VMEM((latent // LANE, seqs * heads, LANE), F32),
            pltpu.VMEM((seqs, heads * latent), BF16),
            pltpu.VMEM((tok_dev, width), BF16),
            pltpu.SemaphoreType.DMA((STAGES, WAVES, len(PARTS))),
            pltpu.SemaphoreType.DMA((STAGES, WAVES, len(PARTS))),
            pltpu.SemaphoreType.DMA((2 + len(PARTS) + 5 + 2,)),
            pltpu.SemaphoreType.DMA((3,)),
        ]
    )
    results = pl.pallas_call(
        kernel,
        out_shape=(
            jax.ShapeDtypeStruct((tok_dev, width), BF16),
            jax.ShapeDtypeStruct((seqs, heads * latent), BF16),
        ),
        in_specs=[pl.BlockSpec(memory_space=pl.ANY)] * 11,
        out_specs=[pl.BlockSpec(memory_space=pl.ANY)] * 2,
        scratch_shapes=scratch,
        compiler_params=pltpu.CompilerParams(
            collective_id=0, has_side_effects=True, vmem_limit_bytes=62 * 1024 * 1024
        ),
    )(tokens, routes.T, affinity.T, w_gate, w_up, w_down, q_latent, q_rope, cache_latent, cache_rope, lengths)
    anywhere = [pl.BlockSpec(memory_space=pl.ANY)] * 2
    return pl.pallas_call(
        finish,
        out_shape=tuple(jax.ShapeDtypeStruct(x.shape, x.dtype) for x in results),
        in_specs=anywhere,
        out_specs=anywhere,
        scratch_shapes=[pltpu.VMEM(x.shape, x.dtype) for x in results]
        + [pltpu.SemaphoreType.DMA((3,)), pltpu.SemaphoreType.DMA((3,))],
        compiler_params=pltpu.CompilerParams(vmem_limit_bytes=62 * 1024 * 1024),
    )(*results)


def finish(moe_in, attn_in, moe_out, attn_out, moe_v, attn_v, in_sem, out_sem):
    half = attn_in.shape[1] // 2
    pieces = [(moe_in, moe_v, moe_out)]
    for i in range(2):
        pieces.append(tuple(ref.at[:, pl.ds(i * half, half)] for ref in (attn_in, attn_v, attn_out)))
    first = [pltpu.make_async_copy(src, mid, in_sem.at[i]) for i, (src, mid, _) in enumerate(pieces)]
    last = [pltpu.make_async_copy(mid, dst, out_sem.at[i]) for i, (_, mid, dst) in enumerate(pieces)]
    for copy in first:
        copy.start()
    for copy, then in zip(first, last):
        copy.wait()
        then.start()
    for copy in last:
        copy.wait()


def solution(mesh):
    rows = P(("group", "member"), None)
    cube = P(("group", "member"), None, None)
    return jax.shard_map(
        per_device,
        mesh=mesh,
        in_specs=(rows, rows, rows, cube, cube, cube, cube, rows, cube, cube, P(("group", "member"))),
        out_specs=(rows, rows),
        check_vma=False,
    )
```

```python
import functools

import jax
import jax.numpy as jnp
from jax import lax
from jax.experimental import pallas as pl
from jax.experimental.pallas import tpu as pltpu
from jax.sharding import PartitionSpec as P

MESH = pl.DeviceIdType.MESH
F32 = jnp.float32
BF16 = jnp.bfloat16

ROTATIONS = (("z", "x", "y"), ("x", "y", "z"), ("y", "z", "x"))
TILES = ((9, 10, 9),)
LANE = 128
SIDE = 4
TOK = 16
SLOTS = 2
LINE = 2 * SIDE
SOURCES = SIDE * SIDE
WAVES = 2
FEW = SOURCES // WAVES
HELD = FEW * TOK
BLOCK = FEW * SLOTS
ROWS = LINE * BLOCK
GATHER_A, GATHER_B, TO_EXPERT, FROM_EXPERT, SUM_B, SUM_A, CODE_A, CODE_B = range(8)
STAGES = 8
ATTEND = (2, 2, 2)
qk_scale = 192.0 ** (-0.5)
route_scale = 2.5


def columns():
    table, start = [], 0
    for chunk in TILES:
        row = []
        for tiles in chunk:
            row.append((start * LANE, tiles * LANE))
            start += tiles
        table.append(row)
    return table


COLS = columns()
CHUNKS = len(TILES)
PARTS = [(c, r) for c in range(CHUNKS) for r in range(3)]


def dot(a, b):
    return jnp.dot(a, b, preferred_element_type=F32)


def dot_nt(a, b):
    return lax.dot_general(a, b, (((1,), (1,)), ((), ())), preferred_element_type=F32)


def rows_at(index, size):
    return pl.ds(pl.multiple_of(index * size, size), size)


def iota(shape, dim):
    return lax.broadcasted_iota(jnp.int32, shape, dim)


def order_of(rotation, digits):
    a, b, c = ROTATIONS[rotation]
    place = digits[b] * (SIDE // 2) + digits[a] // 2
    return (digits[c] * 2 + digits["core"]) * BLOCK + digits["slot"] * FEW + place


def digits_of(rotation, wave, index):
    a, b, c = ROTATIONS[rotation]
    found = {
        c: index // (2 * BLOCK),
        "core": (index // BLOCK) % 2,
        "slot": (index // FEW) % SLOTS,
        b: (index // 2) % SIDE,
    }
    found[a] = 2 * (index % 2) + (found[b] + found[c] + wave) % 2
    return found


def kernel(
    tokens, routes, affinity, w_gate, w_up, w_down, q_latent, q_rope, cache_latent, cache_rope, lengths,
    moe_out, attn_out,
    *scratch,
):
    it = iter(scratch)

    def take():
        return [[next(it) for _ in range(3)] for _ in range(CHUNKS)]

    held = take()
    send, recv, result, back, part, sum_b, both_b = ([take() for _ in range(WAVES)] for _ in range(7))
    sum_a = take()
    codes_v = [next(it) for _ in range(3)]
    aligned, hidden, hidden_r, weigh, perm = (next(it) for _ in range(5))
    routes_v, affinity_v, gate_v, up_v, down_v = (next(it) for _ in range(5))
    ql_v, qr_v, cl_v, cr_v, len_s, q_heads, att, attn_v, moe_v = (next(it) for _ in range(9))
    send_sem, recv_sem, local_sem, weight_sem = (next(it) for _ in range(4))

    group, member = lax.axis_index("group"), lax.axis_index("member")
    me = {"z": group // 2, "core": group % 2, "x": member // 4, "y": member % 4}

    def device(**other):
        at = dict(me)
        at.update(other)
        return (at["z"] * 2 + at["core"], at["x"] * 4 + at["y"])

    barrier = pltpu.get_barrier_semaphore()
    other_core = 1 - me["core"]
    pl.semaphore_signal(barrier, inc=1, device_id=device(core=other_core), device_id_type=MESH)
    for axis in "zxy":
        for k in (1, 3, 2):
            place = (me[axis] + k) % SIDE
            for core in (me["core"], other_core):
                pl.semaphore_signal(barrier, inc=1, device_id=device(**{axis: place, "core": core}), device_id_type=MESH)

    parity = (me["x"] + me["y"] + me["z"]) % 2

    def slot_of(r, a_place):
        return rows_at(me[ROTATIONS[r][1]] * 2 + a_place // 2, TOK)

    def own_slot(r):
        return slot_of(r, me[ROTATIONS[r][0]])

    local = []

    def bring(src, dst):
        copy = pltpu.make_async_copy(src, dst, local_sem.at[len(local)])
        copy.start()
        local.append(copy)
        return copy

    small = [bring(routes, routes_v), bring(affinity, affinity_v)]
    token_copies = []
    for c, r in PARTS:
        start, width = COLS[c][r]
        token_copies.append(bring(tokens.at[:, pl.ds(start, width)], held[c][r].at[parity, own_slot(r)]))
    attention_copies = [bring(q_rope, qr_v), bring(q_latent, ql_v), bring(cache_latent, cl_v), bring(cache_rope, cr_v), bring(lengths, len_s)]
    weight_copies = []
    for number, (src, dst) in enumerate(((w_gate, gate_v), (w_up, up_v), (w_down, down_v))):
        weight_copies.append(pltpu.make_async_copy(src.at[0], dst, weight_sem.at[number]))

    def remote(src, dst, stage, wave, c, r, to):
        part_of = c * 3 + r
        return pltpu.make_async_remote_copy(
            src_ref=src, dst_ref=dst,
            send_sem=send_sem.at[stage, wave, part_of], recv_sem=recv_sem.at[stage, wave, part_of],
            device_id=to, device_id_type=MESH,
        )

    def await_rows(ref, rows, sem, stage, wave, c, r):
        some = ref.at[pl.ds(0, rows)]
        pltpu.make_async_copy(some, some, sem.at[stage, wave, c * 3 + r]).wait()

    for copy in token_copies:
        copy.wait()
    seqs, heads, latent = ql_v.shape
    rope = cr_v.shape[1]
    cached = cr_v.shape[2]

    def split_heads(p, _):
        pair = qr_v[:, pl.ds(pl.multiple_of(p * LANE, LANE), LANE)].astype(F32)
        q_heads[pl.ds(2 * p, seqs, stride=heads), :] = pair
        q_heads[pl.ds(2 * p + 1, seqs, stride=heads), :] = pltpu.roll(pair, LANE - rope, 1)
        return 0

    def attend(s, _):
        q_rot = q_heads[rows_at(s, heads), :][:, :rope].astype(BF16)
        keys = cl_v[s]
        scores = (dot_nt(ql_v[s], keys) + dot(q_rot, cr_v[s])) * qk_scale
        valid = iota((heads, cached), 1) < len_s[s]
        scores = jnp.where(valid, scores, -1e30)
        top = jnp.max(scores, axis=1, keepdims=True)
        expo = jnp.where(valid, jnp.exp(scores - top), 0.0)
        probs = (expo / jnp.sum(expo, axis=1, keepdims=True)).astype(BF16)
        mixed = dot(probs, keys)
        for q in range(latent // LANE):
            att[q, rows_at(s, heads), :] = mixed[:, q * LANE : (q + 1) * LANE]
        return 0

    def join_heads(h, _):
        for q in range(latent // LANE):
            lane = pl.ds(pl.multiple_of(h * latent + q * LANE, LANE), LANE)
            attn_v[:, lane] = att[q, pl.ds(h, seqs, stride=heads), :].astype(BF16)
        return 0

    pl.semaphore_wait(barrier, 1 + 3 * 3 * 2)

    def send_own(stage, axis, refs, c, r):
        along = ROTATIONS[r][axis]
        block = refs.at[parity, own_slot(r)]
        for k in (1, 3, 2):
            remote(block, block, stage, parity, c, r, device(**{along: (me[along] + k) % SIDE})).start()

    for c, r in PARTS:
        send_own(GATHER_A, 0, held[c][r], c, r)

    for copy in small:
        copy.wait()
    sig = 1.0 / (1.0 + jnp.exp(-affinity_v[...]))
    weight = route_scale * sig / jnp.sum(sig, axis=0, keepdims=True)
    chosen = routes_v[...]
    expert_row = iota((LANE, TOK), 0)
    dense = jnp.zeros((LANE, TOK), F32)
    hit = jnp.zeros((LANE, TOK), F32)
    for j in range(chosen.shape[0]):
        same = chosen[j : j + 1, :] == expert_row
        dense = jnp.where(same, weight[j : j + 1, :], dense)
        hit = jnp.where(same, 1.0, hit)
    before = jnp.where(iota((TOK, TOK), 0) < iota((TOK, TOK), 1), 1.0, 0.0).astype(BF16)
    rank = dot(hit.astype(BF16), before)
    signed = jnp.where(rank > 0.5, -dense, dense)
    code = jnp.concatenate([signed, jnp.zeros((LANE, LANE - TOK), F32)], axis=1).T[:TOK].astype(BF16)
    for r in range(3):
        codes_v[r][parity, own_slot(r), :] = code

    for c, r in PARTS:
        send_own(GATHER_B, 1, held[c][r], c, r)
    for r in range(3):
        send_own(CODE_A, 0, codes_v[r], 0, r)
    for r in range(3):
        send_own(CODE_B, 1, codes_v[r], 0, r)
    for copy in attention_copies:
        copy.wait()
    for copy in weight_copies:
        copy.start()
    lax.fori_loop(0, heads // 2, split_heads, 0, unroll=8)

    lax.fori_loop(0, ATTEND[0], attend, 0, unroll=True)

    for wave in range(WAVES):
        for r in (1, 2):
            here = order_of(r, digits_of(0, wave, iota((ROWS, ROWS), 0)))
            perm[wave, :, pl.ds((r - 1) * ROWS, ROWS)] = jnp.where(here == iota((ROWS, ROWS), 1), 1.0, 0.0).astype(BF16)

    lax.fori_loop(ATTEND[0], ATTEND[0] + ATTEND[1], attend, 0, unroll=True)

    def pass_on(refs, stages, wave, c, r):
        a, b, _ = ROTATIONS[r]
        mine = refs.at[wave]
        far = mine.at[slot_of(r, (me[a] + 2) % SIDE)]
        both = mine.at[rows_at(me[b], 2 * TOK)]

        @pl.when(parity == wave)
        def _():
            await_rows(mine, TOK, recv_sem, stages[0], wave, c, r)
            for k in (1, 3, 2):
                remote(far, far, stages[1], wave, c, r, device(**{b: (me[b] + k) % SIDE})).start()

        @pl.when(parity != wave)
        def _():
            await_rows(mine, 2 * TOK, recv_sem, stages[0], wave, c, r)
            for k in (1, 3, 2):
                remote(both, both, stages[1], wave, c, r, device(**{b: (me[b] + k) % SIDE})).start()

    for wave in range(WAVES):
        for c, r in PARTS:
            pass_on(held[c][r], (GATHER_A, GATHER_B), wave, c, r)
        for r in range(3):
            pass_on(codes_v[r], (CODE_A, CODE_B), wave, 0, r)
        if wave == 0:
            lax.fori_loop(ATTEND[0] + ATTEND[1], sum(ATTEND), attend, 0, unroll=True)

    place = iota((BLOCK, HELD), 0)
    own_source = place % FEW == iota((BLOCK, HELD), 1) // TOK
    slot_sign = jnp.where(place < FEW, 1.0, -1.0)
    line_order = ((1, 0), (3, 1), (2, 0), (3, 0), (1, 1), (2, 1), (0, 1))

    def own_block(r):
        return rows_at(me[ROTATIONS[r][2]] * 2 + me["core"], BLOCK)

    def line_peer(r, k, flip):
        c_axis = ROTATIONS[r][2]
        at, core = (me[c_axis] + k) % SIDE, (me["core"] + flip) % 2
        return rows_at(at * 2 + core, BLOCK), device(**{c_axis: at, "core": core})

    def exchange(outgoing, incoming, stage, wave, c, r):
        for k, flip in line_order:
            block, to = line_peer(r, k, flip)
            remote(outgoing.at[block], incoming.at[own_block(r)], stage, wave, c, r, to).start()
        incoming[own_block(r), :] = outgoing[own_block(r), :]

    scaled = {}
    for wave in range(WAVES):
        pick = []
        for r in range(3):
            await_rows(codes_v[r].at[wave], 6 * TOK, recv_sem, CODE_B, wave, 0, r)
            c_axis = ROTATIONS[r][2]
            peer = iota((LINE, LANE), 0)
            at = dict(me)
            at[c_axis] = peer // 2
            expert = (at["z"] * 2 + peer % 2) * 16 + at["x"] * 4 + at["y"]
            select = jnp.where(expert == iota((LINE, LANE), 1), 1.0, 0.0).astype(BF16)
            codes = dot_nt(select, codes_v[r][wave])
            parts = []
            for e in range(LINE):
                signed = codes[e : e + 1, :] * slot_sign
                parts.append(jnp.where(jnp.logical_and(own_source, signed > 0.0), signed, 0.0))
            scaled[wave, r] = jnp.concatenate(parts, axis=0)
            pick.append(jnp.where(scaled[wave, r] > 0.0, 1.0, 0.0).astype(BF16))
        for c in range(CHUNKS):
            for r in range(3):
                await_rows(held[c][r].at[wave], 6 * TOK, recv_sem, GATHER_B, wave, c, r)
            for r in range(3):
                send[wave][c][r][...] = dot(pick[r], held[c][r][wave]).astype(BF16)
            for r in range(3):
                exchange(send[wave][c][r], recv[wave][c][r], TO_EXPERT, wave, c, r)
    for wave in range(WAVES):
        for r in range(3):
            weigh[wave, r] = scaled[wave, r].T.astype(BF16)

    pair = 2 * TOK

    def combine(wave, c, r):
        b = ROTATIONS[r][1]
        await_rows(back[wave][c][r], ROWS - BLOCK, recv_sem, FROM_EXPERT, wave, c, r)
        mine = part[wave][c][r]
        mine[...] = dot(weigh[wave, r], back[wave][c][r][...]).astype(BF16)
        own = rows_at(me[b], pair)
        for k in (1, 3, 2):
            to = (me[b] + k) % SIDE
            remote(mine.at[rows_at(to, pair)], sum_b[wave][c][r].at[own], SUM_B, wave, c, r, device(**{b: to})).start()
        sum_b[wave][c][r][own, :] = mine[own, :]

    ff = gate_v.shape[1]
    step = 512
    for wave in range(WAVES):
        for c, r in PARTS:
            await_rows(recv[wave][c][r], ROWS - BLOCK, recv_sem, TO_EXPERT, wave, c, r)
        for c, r in PARTS:
            start, width = COLS[c][r]
            if r == 0:
                aligned[:, pl.ds(start, width)] = recv[wave][c][r][...]
            else:
                aligned[:, pl.ds(start, width)] = dot(perm[wave, :, pl.ds((r - 1) * ROWS, ROWS)], recv[wave][c][r][...]).astype(BF16)
        if wave == 0:
            for copy in weight_copies:
                copy.wait()

        def ff_tile(n, _):
            tile = pl.ds(pl.multiple_of(n * step, step), step)
            gate = dot(aligned[...], gate_v[:, tile])
            upper = dot(aligned[...], up_v[:, tile])
            hidden[:, tile] = (gate / (1.0 + jnp.exp(-gate)) * upper).astype(BF16)
            return 0

        lax.fori_loop(0, ff // step, ff_tile, 0, unroll=True)
        hidden_r[...] = lax.dot_general(
            perm[wave], hidden[...], (((0,), (0,)), ((), ())), preferred_element_type=F32
        ).astype(BF16)
        for c, r in PARTS:
            start, width = COLS[c][r]
            rows = hidden[...] if r == 0 else hidden_r[pl.ds((r - 1) * ROWS, ROWS), :]
            result[wave][c][r][...] = dot(rows, down_v[:, pl.ds(start, width)]).astype(BF16)
            exchange(result[wave][c][r], back[wave][c][r], FROM_EXPERT, wave, c, r)
    lax.fori_loop(sum(ATTEND), seqs, attend, 0, unroll=True)
    lax.fori_loop(0, heads, join_heads, 0, unroll=8)
    attn_copy = pltpu.make_async_copy(attn_v, attn_out, local_sem.at[len(local)])
    attn_copy.start()

    for wave in range(WAVES):
        for c, r in PARTS:
            combine(wave, c, r)

    for wave in range(WAVES):
        for c, r in PARTS:
            a, b, _ = ROTATIONS[r]
            arrived = sum_b[wave][c][r]
            await_rows(arrived, 3 * pair, recv_sem, SUM_B, wave, c, r)
            total = arrived[pl.ds(0, pair), :].astype(F32)
            for k in range(1, SIDE):
                total = total + arrived[pl.ds(k * pair, pair), :].astype(F32)
            mine = both_b[wave][c][r]
            mine[...] = total.astype(BF16)
            own = rows_at(me[a], TOK)

            def give(to, c=c, r=r, wave=wave, mine=mine, own=own, a=a):
                remote(mine.at[rows_at(to // 2, TOK)], sum_a[c][r].at[own], SUM_A, wave, c, r, device(**{a: to})).start()

            @pl.when(parity == wave)
            def _():
                give((me[a] + 2) % SIDE)
                sum_a[c][r][own, :] = mine[rows_at(me[a] // 2, TOK), :]

            @pl.when(parity != wave)
            def _():
                give((me[a] + 1) % SIDE)
                give((me[a] + 3) % SIDE)

    for c, r in PARTS:
        start, width = COLS[c][r]
        await_rows(sum_a[c][r], 3 * TOK, recv_sem, SUM_A, parity, c, r)
        total = sum_a[c][r][pl.ds(0, TOK), :].astype(F32)
        for k in range(1, SIDE):
            total = total + sum_a[c][r][pl.ds(k * TOK, TOK), :].astype(F32)
        moe_v[:, pl.ds(start, width)] = total.astype(BF16)
    moe_copy = pltpu.make_async_copy(moe_v, moe_out, local_sem.at[len(local) + 1])
    moe_copy.start()

    for c, r in PARTS:
        await_rows(held[c][r].at[0], 3 * TOK, send_sem, GATHER_A, parity, c, r)
        if c == 0:
            await_rows(codes_v[r].at[0], 3 * TOK, send_sem, CODE_A, parity, 0, r)
        for wave in range(WAVES):
            if c == 0:
                await_rows(codes_v[r].at[wave], 6 * TOK, send_sem, CODE_B, wave, 0, r)
            await_rows(back[wave][c][r], ROWS - BLOCK, send_sem, TO_EXPERT, wave, c, r)
            await_rows(back[wave][c][r], ROWS - BLOCK, send_sem, FROM_EXPERT, wave, c, r)
            await_rows(sum_b[wave][c][r], 3 * pair, send_sem, SUM_B, wave, c, r)
            await_rows(held[c][r].at[wave], 6 * TOK, send_sem, GATHER_B, wave, c, r)

            @pl.when(parity == wave)
            def _():
                await_rows(sum_a[c][r], TOK, send_sem, SUM_A, wave, c, r)

            @pl.when(parity != wave)
            def _():
                await_rows(sum_a[c][r], 2 * TOK, send_sem, SUM_A, wave, c, r)
    attn_copy.wait()
    moe_copy.wait()


def per_device(tokens, routes, affinity, w_gate, w_up, w_down, q_latent, q_rope, cache_latent, cache_rope, lengths):
    tok_dev, width = tokens.shape
    ff = w_gate.shape[2]
    seqs, heads, latent = q_latent.shape

    def buffers(rows):
        return [pltpu.VMEM((rows, COLS[c][r][1]), BF16) for c, r in PARTS]

    scratch = (
        [pltpu.VMEM((WAVES, HELD, COLS[c][r][1]), BF16) for c, r in PARTS]
        + buffers(ROWS) * (4 * WAVES)
        + buffers(HELD) * (2 * WAVES)
        + buffers(2 * TOK) * WAVES
        + buffers(SIDE * TOK)
        + [pltpu.VMEM((WAVES, HELD, LANE), BF16)] * 3
        + [
            pltpu.VMEM((ROWS, width), BF16),
            pltpu.VMEM((ROWS, ff), BF16),
            pltpu.VMEM((2 * ROWS, ff), BF16),
            pltpu.VMEM((WAVES, 3, HELD, ROWS), BF16),
            pltpu.VMEM((WAVES, ROWS, 2 * ROWS), BF16),
            pltpu.VMEM(routes.shape[::-1], jnp.int32),
            pltpu.VMEM(affinity.shape[::-1], F32),
            pltpu.VMEM((width, ff), BF16),
            pltpu.VMEM((width, ff), BF16),
            pltpu.VMEM((ff, width), BF16),
            pltpu.VMEM(q_latent.shape, BF16),
            pltpu.VMEM(q_rope.shape, BF16),
            pltpu.VMEM(cache_latent.shape, BF16),
            pltpu.VMEM(cache_rope.shape, BF16),
            pltpu.SMEM(lengths.shape, jnp.int32),
            pltpu.VMEM((seqs * heads, LANE), F32),
            pltpu.VMEM((latent // LANE, seqs * heads, LANE), F32),
            pltpu.VMEM((seqs, heads * latent), BF16),
            pltpu.VMEM((tok_dev, width), BF16),
            pltpu.SemaphoreType.DMA((STAGES, WAVES, len(PARTS))),
            pltpu.SemaphoreType.DMA((STAGES, WAVES, len(PARTS))),
            pltpu.SemaphoreType.DMA((2 + len(PARTS) + 5 + 2,)),
            pltpu.SemaphoreType.DMA((3,)),
        ]
    )
    results = pl.pallas_call(
        kernel,
        out_shape=(
            jax.ShapeDtypeStruct((tok_dev, width), BF16),
            jax.ShapeDtypeStruct((seqs, heads * latent), BF16),
        ),
        in_specs=[pl.BlockSpec(memory_space=pl.ANY)] * 11,
        out_specs=[pl.BlockSpec(memory_space=pl.ANY)] * 2,
        scratch_shapes=scratch,
        compiler_params=pltpu.CompilerParams(
            collective_id=0, has_side_effects=True, vmem_limit_bytes=62 * 1024 * 1024
        ),
    )(tokens, routes.T, affinity.T, w_gate, w_up, w_down, q_latent, q_rope, cache_latent, cache_rope, lengths)
    anywhere = [pl.BlockSpec(memory_space=pl.ANY)] * 2
    return pl.pallas_call(
        finish,
        out_shape=tuple(jax.ShapeDtypeStruct(x.shape, x.dtype) for x in results),
        in_specs=anywhere,
        out_specs=anywhere,
        scratch_shapes=[pltpu.VMEM(x.shape, x.dtype) for x in results]
        + [pltpu.SemaphoreType.DMA((3,)), pltpu.SemaphoreType.DMA((3,))],
        compiler_params=pltpu.CompilerParams(vmem_limit_bytes=62 * 1024 * 1024),
    )(*results)


def finish(moe_in, attn_in, moe_out, attn_out, moe_v, attn_v, in_sem, out_sem):
    half = attn_in.shape[1] // 2
    pieces = [(moe_in, moe_v, moe_out)]
    for i in range(2):
        pieces.append(tuple(ref.at[:, pl.ds(i * half, half)] for ref in (attn_in, attn_v, attn_out)))
    first = [pltpu.make_async_copy(src, mid, in_sem.at[i]) for i, (src, mid, _) in enumerate(pieces)]
    last = [pltpu.make_async_copy(mid, dst, out_sem.at[i]) for i, (_, mid, dst) in enumerate(pieces)]
    for copy in first:
        copy.start()
    for copy, then in zip(first, last):
        copy.wait()
        then.start()
    for copy in last:
        copy.wait()


def solution(mesh):
    rows = P(("group", "member"), None)
    cube = P(("group", "member"), None, None)
    return jax.shard_map(
        per_device,
        mesh=mesh,
        in_specs=(rows, rows, rows, cube, cube, cube, cube, rows, cube, cube, P(("group", "member"))),
        out_specs=(rows, rows),
        check_vma=False,
    )
```

```python
import functools

import jax
import jax.numpy as jnp
from jax import lax
from jax.experimental import pallas as pl
from jax.experimental.pallas import tpu as pltpu
from jax.sharding import PartitionSpec as P

MESH = pl.DeviceIdType.MESH
F32 = jnp.float32
BF16 = jnp.bfloat16

ROTATIONS = (("z", "x", "y"), ("x", "y", "z"), ("y", "z", "x"))
TILES = ((9, 10, 9),)
LANE = 128
SIDE = 4
TOK = 16
SLOTS = 2
LINE = 2 * SIDE
SOURCES = SIDE * SIDE
WAVES = 2
FEW = SOURCES // WAVES
HELD = FEW * TOK
BLOCK = FEW * SLOTS
ROWS = LINE * BLOCK
GATHER_A, GATHER_B, TO_EXPERT, FROM_EXPERT, SUM_B, SUM_A, CODE_A, CODE_B = range(8)
STAGES = 8
ATTEND = (2, 2, 2)
qk_scale = 192.0 ** (-0.5)
route_scale = 2.5


def columns():
    table, start = [], 0
    for chunk in TILES:
        row = []
        for tiles in chunk:
            row.append((start * LANE, tiles * LANE))
            start += tiles
        table.append(row)
    return table


COLS = columns()
CHUNKS = len(TILES)
PARTS = [(c, r) for c in range(CHUNKS) for r in range(3)]


def dot(a, b):
    return jnp.dot(a, b, preferred_element_type=F32)


def dot_nt(a, b):
    return lax.dot_general(a, b, (((1,), (1,)), ((), ())), preferred_element_type=F32)


def rows_at(index, size):
    return pl.ds(pl.multiple_of(index * size, size), size)


def iota(shape, dim):
    return lax.broadcasted_iota(jnp.int32, shape, dim)


def order_of(rotation, digits):
    a, b, c = ROTATIONS[rotation]
    place = digits[b] * (SIDE // 2) + digits[a] // 2
    return (digits[c] * 2 + digits["core"]) * BLOCK + digits["slot"] * FEW + place


def digits_of(rotation, wave, index):
    a, b, c = ROTATIONS[rotation]
    found = {
        c: index // (2 * BLOCK),
        "core": (index // BLOCK) % 2,
        "slot": (index // FEW) % SLOTS,
        b: (index // 2) % SIDE,
    }
    found[a] = 2 * (index % 2) + (found[b] + found[c] + wave) % 2
    return found


def kernel(
    tokens, routes, affinity, w_gate, w_up, w_down, q_latent, q_rope, cache_latent, cache_rope, lengths,
    moe_out, attn_out,
    *scratch,
):
    it = iter(scratch)

    def take():
        return [[next(it) for _ in range(3)] for _ in range(CHUNKS)]

    held = take()
    send, recv, result, back, part, sum_b, both_b = ([take() for _ in range(WAVES)] for _ in range(7))
    sum_a = take()
    codes_v = [next(it) for _ in range(3)]
    aligned, hidden, hidden_r, weigh, perm = (next(it) for _ in range(5))
    routes_v, affinity_v, gate_v, up_v, down_v = (next(it) for _ in range(5))
    ql_v, qr_v, cl_v, cr_v, len_s, q_heads, att, attn_v, moe_v = (next(it) for _ in range(9))
    send_sem, recv_sem, local_sem, weight_sem = (next(it) for _ in range(4))

    group, member = lax.axis_index("group"), lax.axis_index("member")
    me = {"z": group // 2, "core": group % 2, "x": member // 4, "y": member % 4}

    def device(**other):
        at = dict(me)
        at.update(other)
        return (at["z"] * 2 + at["core"], at["x"] * 4 + at["y"])

    barrier = pltpu.get_barrier_semaphore()
    other_core = 1 - me["core"]
    pl.semaphore_signal(barrier, inc=1, device_id=device(core=other_core), device_id_type=MESH)
    for axis in "zxy":
        for k in (1, 3, 2):
            place = (me[axis] + k) % SIDE
            for core in (me["core"], other_core):
                pl.semaphore_signal(barrier, inc=1, device_id=device(**{axis: place, "core": core}), device_id_type=MESH)

    parity = (me["x"] + me["y"] + me["z"]) % 2

    def slot_of(r, a_place):
        return rows_at(me[ROTATIONS[r][1]] * 2 + a_place // 2, TOK)

    def own_slot(r):
        return slot_of(r, me[ROTATIONS[r][0]])

    local = []

    def bring(src, dst):
        copy = pltpu.make_async_copy(src, dst, local_sem.at[len(local)])
        copy.start()
        local.append(copy)
        return copy

    small = [bring(routes, routes_v), bring(affinity, affinity_v)]
    token_copies = []
    for c, r in PARTS:
        start, width = COLS[c][r]
        token_copies.append(bring(tokens.at[:, pl.ds(start, width)], held[c][r].at[parity, own_slot(r)]))
    attention_copies = [bring(q_rope, qr_v), bring(q_latent, ql_v), bring(cache_latent, cl_v), bring(cache_rope, cr_v), bring(lengths, len_s)]
    weight_copies = []
    for number, (src, dst) in enumerate(((w_gate, gate_v), (w_up, up_v), (w_down, down_v))):
        weight_copies.append(pltpu.make_async_copy(src.at[0], dst, weight_sem.at[number]))

    def remote(src, dst, stage, wave, c, r, to):
        part_of = c * 3 + r
        return pltpu.make_async_remote_copy(
            src_ref=src, dst_ref=dst,
            send_sem=send_sem.at[stage, wave, part_of], recv_sem=recv_sem.at[stage, wave, part_of],
            device_id=to, device_id_type=MESH,
        )

    def await_rows(ref, rows, sem, stage, wave, c, r):
        some = ref.at[pl.ds(0, rows)]
        pltpu.make_async_copy(some, some, sem.at[stage, wave, c * 3 + r]).wait()

    seqs, heads, latent = ql_v.shape
    rope = cr_v.shape[1]
    cached = cr_v.shape[2]

    def split_heads(p, _):
        pair = qr_v[:, pl.ds(pl.multiple_of(p * LANE, LANE), LANE)].astype(F32)
        q_heads[pl.ds(2 * p, seqs, stride=heads), :] = pair
        q_heads[pl.ds(2 * p + 1, seqs, stride=heads), :] = pltpu.roll(pair, LANE - rope, 1)
        return 0

    def attend(s, _):
        q_rot = q_heads[rows_at(s, heads), :][:, :rope].astype(BF16)
        keys = cl_v[s]
        scores = (dot_nt(ql_v[s], keys) + dot(q_rot, cr_v[s])) * qk_scale
        valid = iota((heads, cached), 1) < len_s[s]
        scores = jnp.where(valid, scores, -1e30)
        top = jnp.max(scores, axis=1, keepdims=True)
        expo = jnp.where(valid, jnp.exp(scores - top), 0.0)
        probs = (expo / jnp.sum(expo, axis=1, keepdims=True)).astype(BF16)
        mixed = dot(probs, keys)
        for q in range(latent // LANE):
            att[q, rows_at(s, heads), :] = mixed[:, q * LANE : (q + 1) * LANE]
        return 0

    def join_heads(h, _):
        for q in range(latent // LANE):
            lane = pl.ds(pl.multiple_of(h * latent + q * LANE, LANE), LANE)
            attn_v[:, lane] = att[q, pl.ds(h, seqs, stride=heads), :].astype(BF16)
        return 0

    pl.semaphore_wait(barrier, 1 + 3 * 3 * 2)

    def send_own(stage, axis, src, refs, c, r):
        along = ROTATIONS[r][axis]
        block = refs.at[parity, own_slot(r)]
        for k in (1, 3, 2):
            remote(src, block, stage, parity, c, r, device(**{along: (me[along] + k) % SIDE})).start()

    for c, r in PARTS:
        send_own(GATHER_A, 0, tokens.at[:, pl.ds(*COLS[c][r])], held[c][r], c, r)

    for copy in small:
        copy.wait()
    sig = 1.0 / (1.0 + jnp.exp(-affinity_v[...]))
    weight = route_scale * sig / jnp.sum(sig, axis=0, keepdims=True)
    chosen = routes_v[...]
    expert_row = iota((LANE, TOK), 0)
    dense = jnp.zeros((LANE, TOK), F32)
    hit = jnp.zeros((LANE, TOK), F32)
    for j in range(chosen.shape[0]):
        same = chosen[j : j + 1, :] == expert_row
        dense = jnp.where(same, weight[j : j + 1, :], dense)
        hit = jnp.where(same, 1.0, hit)
    before = jnp.where(iota((TOK, TOK), 0) < iota((TOK, TOK), 1), 1.0, 0.0).astype(BF16)
    rank = dot(hit.astype(BF16), before)
    signed = jnp.where(rank > 0.5, -dense, dense)
    code = jnp.concatenate([signed, jnp.zeros((LANE, LANE - TOK), F32)], axis=1).T[:TOK].astype(BF16)
    for r in range(3):
        codes_v[r][parity, own_slot(r), :] = code

    for c, r in PARTS:
        send_own(GATHER_B, 1, tokens.at[:, pl.ds(*COLS[c][r])], held[c][r], c, r)
    for r in range(3):
        send_own(CODE_A, 0, codes_v[r].at[parity, own_slot(r)], codes_v[r], 0, r)
    for r in range(3):
        send_own(CODE_B, 1, codes_v[r].at[parity, own_slot(r)], codes_v[r], 0, r)
    for copy in token_copies + attention_copies:
        copy.wait()
    for copy in weight_copies:
        copy.start()
    lax.fori_loop(0, heads // 2, split_heads, 0, unroll=8)

    lax.fori_loop(0, ATTEND[0], attend, 0, unroll=True)

    for wave in range(WAVES):
        for r in (1, 2):
            here = order_of(r, digits_of(0, wave, iota((ROWS, ROWS), 0)))
            perm[wave, :, pl.ds((r - 1) * ROWS, ROWS)] = jnp.where(here == iota((ROWS, ROWS), 1), 1.0, 0.0).astype(BF16)

    lax.fori_loop(ATTEND[0], ATTEND[0] + ATTEND[1], attend, 0, unroll=True)

    def pass_on(refs, stages, wave, c, r):
        a, b, _ = ROTATIONS[r]
        mine = refs.at[wave]
        far = mine.at[slot_of(r, (me[a] + 2) % SIDE)]
        both = mine.at[rows_at(me[b], 2 * TOK)]

        @pl.when(parity == wave)
        def _():
            await_rows(mine, TOK, recv_sem, stages[0], wave, c, r)
            for k in (1, 3, 2):
                remote(far, far, stages[1], wave, c, r, device(**{b: (me[b] + k) % SIDE})).start()

        @pl.when(parity != wave)
        def _():
            await_rows(mine, 2 * TOK, recv_sem, stages[0], wave, c, r)
            for k in (1, 3, 2):
                remote(both, both, stages[1], wave, c, r, device(**{b: (me[b] + k) % SIDE})).start()

    for wave in range(WAVES):
        for c, r in PARTS:
            pass_on(held[c][r], (GATHER_A, GATHER_B), wave, c, r)
        for r in range(3):
            pass_on(codes_v[r], (CODE_A, CODE_B), wave, 0, r)
        if wave == 0:
            lax.fori_loop(ATTEND[0] + ATTEND[1], sum(ATTEND), attend, 0, unroll=True)

    place = iota((BLOCK, HELD), 0)
    own_source = place % FEW == iota((BLOCK, HELD), 1) // TOK
    slot_sign = jnp.where(place < FEW, 1.0, -1.0)
    line_order = ((1, 0), (3, 1), (2, 0), (3, 0), (1, 1), (2, 1), (0, 1))

    def own_block(r):
        return rows_at(me[ROTATIONS[r][2]] * 2 + me["core"], BLOCK)

    def line_peer(r, k, flip):
        c_axis = ROTATIONS[r][2]
        at, core = (me[c_axis] + k) % SIDE, (me["core"] + flip) % 2
        return rows_at(at * 2 + core, BLOCK), device(**{c_axis: at, "core": core})

    def exchange(outgoing, incoming, stage, wave, c, r):
        for k, flip in line_order:
            block, to = line_peer(r, k, flip)
            remote(outgoing.at[block], incoming.at[own_block(r)], stage, wave, c, r, to).start()
        incoming[own_block(r), :] = outgoing[own_block(r), :]

    scaled = {}
    for wave in range(WAVES):
        pick = []
        for r in range(3):
            await_rows(codes_v[r].at[wave], 6 * TOK, recv_sem, CODE_B, wave, 0, r)
            c_axis = ROTATIONS[r][2]
            peer = iota((LINE, LANE), 0)
            at = dict(me)
            at[c_axis] = peer // 2
            expert = (at["z"] * 2 + peer % 2) * 16 + at["x"] * 4 + at["y"]
            select = jnp.where(expert == iota((LINE, LANE), 1), 1.0, 0.0).astype(BF16)
            codes = dot_nt(select, codes_v[r][wave])
            parts = []
            for e in range(LINE):
                signed = codes[e : e + 1, :] * slot_sign
                parts.append(jnp.where(jnp.logical_and(own_source, signed > 0.0), signed, 0.0))
            scaled[wave, r] = jnp.concatenate(parts, axis=0)
            pick.append(jnp.where(scaled[wave, r] > 0.0, 1.0, 0.0).astype(BF16))
        for c in range(CHUNKS):
            for r in range(3):
                await_rows(held[c][r].at[wave], 6 * TOK, recv_sem, GATHER_B, wave, c, r)
            for r in range(3):
                send[wave][c][r][...] = dot(pick[r], held[c][r][wave]).astype(BF16)
            for r in range(3):
                exchange(send[wave][c][r], recv[wave][c][r], TO_EXPERT, wave, c, r)
    for wave in range(WAVES):
        for r in range(3):
            weigh[wave, r] = scaled[wave, r].T.astype(BF16)

    pair = 2 * TOK

    def combine(wave, c, r):
        b = ROTATIONS[r][1]
        await_rows(back[wave][c][r], ROWS - BLOCK, recv_sem, FROM_EXPERT, wave, c, r)
        mine = part[wave][c][r]
        mine[...] = dot(weigh[wave, r], back[wave][c][r][...]).astype(BF16)
        own = rows_at(me[b], pair)
        for k in (1, 3, 2):
            to = (me[b] + k) % SIDE
            remote(mine.at[rows_at(to, pair)], sum_b[wave][c][r].at[own], SUM_B, wave, c, r, device(**{b: to})).start()
        sum_b[wave][c][r][own, :] = mine[own, :]

    ff = gate_v.shape[1]
    step = 512
    for wave in range(WAVES):
        for c, r in PARTS:
            await_rows(recv[wave][c][r], ROWS - BLOCK, recv_sem, TO_EXPERT, wave, c, r)
        for c, r in PARTS:
            start, width = COLS[c][r]
            if r == 0:
                aligned[:, pl.ds(start, width)] = recv[wave][c][r][...]
            else:
                aligned[:, pl.ds(start, width)] = dot(perm[wave, :, pl.ds((r - 1) * ROWS, ROWS)], recv[wave][c][r][...]).astype(BF16)
        if wave == 0:
            for copy in weight_copies:
                copy.wait()

        def ff_tile(n, _):
            tile = pl.ds(pl.multiple_of(n * step, step), step)
            gate = dot(aligned[...], gate_v[:, tile])
            upper = dot(aligned[...], up_v[:, tile])
            hidden[:, tile] = (gate / (1.0 + jnp.exp(-gate)) * upper).astype(BF16)
            return 0

        lax.fori_loop(0, ff // step, ff_tile, 0, unroll=True)
        hidden_r[...] = lax.dot_general(
            perm[wave], hidden[...], (((0,), (0,)), ((), ())), preferred_element_type=F32
        ).astype(BF16)
        for c, r in PARTS:
            start, width = COLS[c][r]
            rows = hidden[...] if r == 0 else hidden_r[pl.ds((r - 1) * ROWS, ROWS), :]
            result[wave][c][r][...] = dot(rows, down_v[:, pl.ds(start, width)]).astype(BF16)
            exchange(result[wave][c][r], back[wave][c][r], FROM_EXPERT, wave, c, r)
    lax.fori_loop(sum(ATTEND), seqs, attend, 0, unroll=True)
    lax.fori_loop(0, heads, join_heads, 0, unroll=8)
    attn_copy = pltpu.make_async_copy(attn_v, attn_out, local_sem.at[len(local)])
    attn_copy.start()

    for wave in range(WAVES):
        for c, r in PARTS:
            combine(wave, c, r)

    for wave in range(WAVES):
        for c, r in PARTS:
            a, b, _ = ROTATIONS[r]
            arrived = sum_b[wave][c][r]
            await_rows(arrived, 3 * pair, recv_sem, SUM_B, wave, c, r)
            total = arrived[pl.ds(0, pair), :].astype(F32)
            for k in range(1, SIDE):
                total = total + arrived[pl.ds(k * pair, pair), :].astype(F32)
            mine = both_b[wave][c][r]
            mine[...] = total.astype(BF16)
            own = rows_at(me[a], TOK)

            def give(to, c=c, r=r, wave=wave, mine=mine, own=own, a=a):
                remote(mine.at[rows_at(to // 2, TOK)], sum_a[c][r].at[own], SUM_A, wave, c, r, device(**{a: to})).start()

            @pl.when(parity == wave)
            def _():
                give((me[a] + 2) % SIDE)
                sum_a[c][r][own, :] = mine[rows_at(me[a] // 2, TOK), :]

            @pl.when(parity != wave)
            def _():
                give((me[a] + 1) % SIDE)
                give((me[a] + 3) % SIDE)

    for c, r in PARTS:
        start, width = COLS[c][r]
        await_rows(sum_a[c][r], 3 * TOK, recv_sem, SUM_A, parity, c, r)
        total = sum_a[c][r][pl.ds(0, TOK), :].astype(F32)
        for k in range(1, SIDE):
            total = total + sum_a[c][r][pl.ds(k * TOK, TOK), :].astype(F32)
        moe_v[:, pl.ds(start, width)] = total.astype(BF16)
    moe_copy = pltpu.make_async_copy(moe_v, moe_out, local_sem.at[len(local) + 1])
    moe_copy.start()

    for c, r in PARTS:
        await_rows(held[c][r].at[0], 3 * TOK, send_sem, GATHER_A, parity, c, r)
        if c == 0:
            await_rows(codes_v[r].at[0], 3 * TOK, send_sem, CODE_A, parity, 0, r)
        for wave in range(WAVES):
            if c == 0:
                await_rows(codes_v[r].at[wave], 6 * TOK, send_sem, CODE_B, wave, 0, r)
            await_rows(back[wave][c][r], ROWS - BLOCK, send_sem, TO_EXPERT, wave, c, r)
            await_rows(back[wave][c][r], ROWS - BLOCK, send_sem, FROM_EXPERT, wave, c, r)
            await_rows(sum_b[wave][c][r], 3 * pair, send_sem, SUM_B, wave, c, r)
            await_rows(held[c][r].at[wave], 6 * TOK, send_sem, GATHER_B, wave, c, r)

            @pl.when(parity == wave)
            def _():
                await_rows(sum_a[c][r], TOK, send_sem, SUM_A, wave, c, r)

            @pl.when(parity != wave)
            def _():
                await_rows(sum_a[c][r], 2 * TOK, send_sem, SUM_A, wave, c, r)
    attn_copy.wait()
    moe_copy.wait()


def per_device(tokens, routes, affinity, w_gate, w_up, w_down, q_latent, q_rope, cache_latent, cache_rope, lengths):
    tok_dev, width = tokens.shape
    ff = w_gate.shape[2]
    seqs, heads, latent = q_latent.shape

    def buffers(rows):
        return [pltpu.VMEM((rows, COLS[c][r][1]), BF16) for c, r in PARTS]

    scratch = (
        [pltpu.VMEM((WAVES, HELD, COLS[c][r][1]), BF16) for c, r in PARTS]
        + buffers(ROWS) * (4 * WAVES)
        + buffers(HELD) * (2 * WAVES)
        + buffers(2 * TOK) * WAVES
        + buffers(SIDE * TOK)
        + [pltpu.VMEM((WAVES, HELD, LANE), BF16)] * 3
        + [
            pltpu.VMEM((ROWS, width), BF16),
            pltpu.VMEM((ROWS, ff), BF16),
            pltpu.VMEM((2 * ROWS, ff), BF16),
            pltpu.VMEM((WAVES, 3, HELD, ROWS), BF16),
            pltpu.VMEM((WAVES, ROWS, 2 * ROWS), BF16),
            pltpu.VMEM(routes.shape[::-1], jnp.int32),
            pltpu.VMEM(affinity.shape[::-1], F32),
            pltpu.VMEM((width, ff), BF16),
            pltpu.VMEM((width, ff), BF16),
            pltpu.VMEM((ff, width), BF16),
            pltpu.VMEM(q_latent.shape, BF16),
            pltpu.VMEM(q_rope.shape, BF16),
            pltpu.VMEM(cache_latent.shape, BF16),
            pltpu.VMEM(cache_rope.shape, BF16),
            pltpu.SMEM(lengths.shape, jnp.int32),
            pltpu.VMEM((seqs * heads, LANE), F32),
            pltpu.VMEM((latent // LANE, seqs * heads, LANE), F32),
            pltpu.VMEM((seqs, heads * latent), BF16),
            pltpu.VMEM((tok_dev, width), BF16),
            pltpu.SemaphoreType.DMA((STAGES, WAVES, len(PARTS))),
            pltpu.SemaphoreType.DMA((STAGES, WAVES, len(PARTS))),
            pltpu.SemaphoreType.DMA((2 + len(PARTS) + 5 + 2,)),
            pltpu.SemaphoreType.DMA((3,)),
        ]
    )
    results = pl.pallas_call(
        kernel,
        out_shape=(
            jax.ShapeDtypeStruct((tok_dev, width), BF16),
            jax.ShapeDtypeStruct((seqs, heads * latent), BF16),
        ),
        in_specs=[pl.BlockSpec(memory_space=pl.ANY)] * 11,
        out_specs=[pl.BlockSpec(memory_space=pl.ANY)] * 2,
        scratch_shapes=scratch,
        compiler_params=pltpu.CompilerParams(
            collective_id=0, has_side_effects=True, vmem_limit_bytes=62 * 1024 * 1024
        ),
    )(tokens, routes.T, affinity.T, w_gate, w_up, w_down, q_latent, q_rope, cache_latent, cache_rope, lengths)
    anywhere = [pl.BlockSpec(memory_space=pl.ANY)] * 2
    return pl.pallas_call(
        finish,
        out_shape=tuple(jax.ShapeDtypeStruct(x.shape, x.dtype) for x in results),
        in_specs=anywhere,
        out_specs=anywhere,
        scratch_shapes=[pltpu.VMEM(x.shape, x.dtype) for x in results]
        + [pltpu.SemaphoreType.DMA((3,)), pltpu.SemaphoreType.DMA((3,))],
        compiler_params=pltpu.CompilerParams(vmem_limit_bytes=62 * 1024 * 1024),
    )(*results)


def finish(moe_in, attn_in, moe_out, attn_out, moe_v, attn_v, in_sem, out_sem):
    half = attn_in.shape[1] // 2
    pieces = [(moe_in, moe_v, moe_out)]
    for i in range(2):
        pieces.append(tuple(ref.at[:, pl.ds(i * half, half)] for ref in (attn_in, attn_v, attn_out)))
    first = [pltpu.make_async_copy(src, mid, in_sem.at[i]) for i, (src, mid, _) in enumerate(pieces)]
    last = [pltpu.make_async_copy(mid, dst, out_sem.at[i]) for i, (_, mid, dst) in enumerate(pieces)]
    for copy in first:
        copy.start()
    for copy, then in zip(first, last):
        copy.wait()
        then.start()
    for copy in last:
        copy.wait()


def solution(mesh):
    rows = P(("group", "member"), None)
    cube = P(("group", "member"), None, None)
    return jax.shard_map(
        per_device,
        mesh=mesh,
        in_specs=(rows, rows, rows, cube, cube, cube, cube, rows, cube, cube, P(("group", "member"))),
        out_specs=(rows, rows),
        check_vma=False,
    )
```

```python
import functools

import jax
import jax.numpy as jnp
from jax import lax
from jax.experimental import pallas as pl
from jax.experimental.pallas import tpu as pltpu
from jax.sharding import PartitionSpec as P

MESH = pl.DeviceIdType.MESH
F32 = jnp.float32
BF16 = jnp.bfloat16

ROTATIONS = (("z", "x", "y"), ("x", "y", "z"), ("y", "z", "x"))
TILES = ((9, 10, 9),)
LANE = 128
SIDE = 4
TOK = 16
SLOTS = 2
LINE = 2 * SIDE
SOURCES = SIDE * SIDE
WAVES = 2
FEW = SOURCES // WAVES
HELD = FEW * TOK
BLOCK = FEW * SLOTS
ROWS = LINE * BLOCK
GATHER_A, GATHER_B, TO_EXPERT, FROM_EXPERT, SUM_B, SUM_A, CODE_A, CODE_B = range(8)
STAGES = 8
ATTEND = (2, 2, 2)
qk_scale = 192.0 ** (-0.5)
route_scale = 2.5


def columns():
    table, start = [], 0
    for chunk in TILES:
        row = []
        for tiles in chunk:
            row.append((start * LANE, tiles * LANE))
            start += tiles
        table.append(row)
    return table


COLS = columns()
CHUNKS = len(TILES)
PARTS = [(c, r) for c in range(CHUNKS) for r in range(3)]


def dot(a, b):
    return jnp.dot(a, b, preferred_element_type=F32)


def dot_nt(a, b):
    return lax.dot_general(a, b, (((1,), (1,)), ((), ())), preferred_element_type=F32)


def rows_at(index, size):
    return pl.ds(pl.multiple_of(index * size, size), size)


def iota(shape, dim):
    return lax.broadcasted_iota(jnp.int32, shape, dim)


def order_of(rotation, digits):
    a, b, c = ROTATIONS[rotation]
    place = digits[b] * (SIDE // 2) + digits[a] // 2
    return (digits[c] * 2 + digits["core"]) * BLOCK + digits["slot"] * FEW + place


def digits_of(rotation, wave, index):
    a, b, c = ROTATIONS[rotation]
    found = {
        c: index // (2 * BLOCK),
        "core": (index // BLOCK) % 2,
        "slot": (index // FEW) % SLOTS,
        b: (index // 2) % SIDE,
    }
    found[a] = 2 * (index % 2) + (found[b] + found[c] + wave) % 2
    return found


def kernel(
    tokens, routes, affinity, w_gate, w_up, w_down, q_latent, q_rope, cache_latent, cache_rope, lengths,
    moe_out, attn_out,
    *scratch,
):
    it = iter(scratch)

    def take():
        return [[next(it) for _ in range(3)] for _ in range(CHUNKS)]

    held = take()
    send, recv, result, back, part, sum_b, both_b = ([take() for _ in range(WAVES)] for _ in range(7))
    sum_a = take()
    codes_v = [next(it) for _ in range(3)]
    aligned, hidden, hidden_r, weigh, perm = (next(it) for _ in range(5))
    routes_v, affinity_v, gate_v, up_v, down_v = (next(it) for _ in range(5))
    ql_v, qr_v, cl_v, cr_v, len_s, q_heads, att, attn_v, moe_v = (next(it) for _ in range(9))
    send_sem, recv_sem, local_sem, weight_sem = (next(it) for _ in range(4))

    group, member = lax.axis_index("group"), lax.axis_index("member")
    me = {"z": group // 2, "core": group % 2, "x": member // 4, "y": member % 4}

    def device(**other):
        at = dict(me)
        at.update(other)
        return (at["z"] * 2 + at["core"], at["x"] * 4 + at["y"])

    barrier = pltpu.get_barrier_semaphore()
    other_core = 1 - me["core"]
    pl.semaphore_signal(barrier, inc=1, device_id=device(core=other_core), device_id_type=MESH)
    for axis in "zxy":
        for k in (1, 3, 2):
            place = (me[axis] + k) % SIDE
            for core in (me["core"], other_core):
                pl.semaphore_signal(barrier, inc=1, device_id=device(**{axis: place, "core": core}), device_id_type=MESH)

    parity = (me["x"] + me["y"] + me["z"]) % 2

    def slot_of(r, a_place):
        return rows_at(me[ROTATIONS[r][1]] * 2 + a_place // 2, TOK)

    def own_slot(r):
        return slot_of(r, me[ROTATIONS[r][0]])

    local = []

    def bring(src, dst):
        copy = pltpu.make_async_copy(src, dst, local_sem.at[len(local)])
        copy.start()
        local.append(copy)
        return copy

    small = [bring(routes, routes_v), bring(affinity, affinity_v)]
    token_copies = []
    for c, r in PARTS:
        start, width = COLS[c][r]
        token_copies.append(bring(tokens.at[:, pl.ds(start, width)], held[c][r].at[parity, own_slot(r)]))
    attention_copies = [bring(q_rope, qr_v), bring(q_latent, ql_v), bring(cache_latent, cl_v), bring(cache_rope, cr_v), bring(lengths, len_s)]
    weight_copies = []
    for number, (src, dst) in enumerate(((w_gate, gate_v), (w_up, up_v), (w_down, down_v))):
        weight_copies.append(pltpu.make_async_copy(src.at[0], dst, weight_sem.at[number]))

    def remote(src, dst, stage, wave, c, r, to):
        part_of = c * 3 + r
        return pltpu.make_async_remote_copy(
            src_ref=src, dst_ref=dst,
            send_sem=send_sem.at[stage, wave, part_of], recv_sem=recv_sem.at[stage, wave, part_of],
            device_id=to, device_id_type=MESH,
        )

    def await_rows(ref, rows, sem, stage, wave, c, r):
        some = ref.at[pl.ds(0, rows)]
        pltpu.make_async_copy(some, some, sem.at[stage, wave, c * 3 + r]).wait()

    seqs, heads, latent = ql_v.shape
    rope = cr_v.shape[1]
    cached = cr_v.shape[2]

    def split_heads(p, _):
        pair = qr_v[:, pl.ds(pl.multiple_of(p * LANE, LANE), LANE)].astype(F32)
        q_heads[pl.ds(2 * p, seqs, stride=heads), :] = pair
        q_heads[pl.ds(2 * p + 1, seqs, stride=heads), :] = pltpu.roll(pair, LANE - rope, 1)
        return 0

    def attend(s, _):
        q_rot = q_heads[rows_at(s, heads), :][:, :rope].astype(BF16)
        keys = cl_v[s]
        scores = (dot_nt(ql_v[s], keys) + dot(q_rot, cr_v[s])) * qk_scale
        valid = iota((heads, cached), 1) < len_s[s]
        scores = jnp.where(valid, scores, -1e30)
        top = jnp.max(scores, axis=1, keepdims=True)
        expo = jnp.where(valid, jnp.exp(scores - top), 0.0)
        probs = (expo / jnp.sum(expo, axis=1, keepdims=True)).astype(BF16)
        mixed = dot(probs, keys)
        for q in range(latent // LANE):
            att[q, rows_at(s, heads), :] = mixed[:, q * LANE : (q + 1) * LANE]
        return 0

    def join_heads(h, _):
        for q in range(latent // LANE):
            lane = pl.ds(pl.multiple_of(h * latent + q * LANE, LANE), LANE)
            attn_v[:, lane] = att[q, pl.ds(h, seqs, stride=heads), :].astype(BF16)
        return 0

    pl.semaphore_wait(barrier, 1 + 3 * 3 * 2)

    def send_own(stage, axis, src, refs, c, r):
        along = ROTATIONS[r][axis]
        block = refs.at[parity, own_slot(r)]
        for k in (1, 3, 2):
            remote(src, block, stage, parity, c, r, device(**{along: (me[along] + k) % SIDE})).start()

    for c, r in PARTS:
        send_own(GATHER_A, 0, tokens.at[:, pl.ds(*COLS[c][r])], held[c][r], c, r)

    for copy in small:
        copy.wait()
    sig = 1.0 / (1.0 + jnp.exp(-affinity_v[...]))
    weight = route_scale * sig / jnp.sum(sig, axis=0, keepdims=True)
    chosen = routes_v[...]
    expert_row = iota((LANE, TOK), 0)
    dense = jnp.zeros((LANE, TOK), F32)
    hit = jnp.zeros((LANE, TOK), F32)
    for j in range(chosen.shape[0]):
        same = chosen[j : j + 1, :] == expert_row
        dense = jnp.where(same, weight[j : j + 1, :], dense)
        hit = jnp.where(same, 1.0, hit)
    before = jnp.where(iota((TOK, TOK), 0) < iota((TOK, TOK), 1), 1.0, 0.0).astype(BF16)
    rank = dot(hit.astype(BF16), before)
    signed = jnp.where(rank > 0.5, -dense, dense)
    code = jnp.concatenate([signed, jnp.zeros((LANE, LANE - TOK), F32)], axis=1).T[:TOK].astype(BF16)
    for r in range(3):
        codes_v[r][parity, own_slot(r), :] = code

    for c, r in PARTS:
        send_own(GATHER_B, 1, tokens.at[:, pl.ds(*COLS[c][r])], held[c][r], c, r)
    for r in range(3):
        send_own(CODE_A, 0, codes_v[r].at[parity, own_slot(r)], codes_v[r], 0, r)
    for r in range(3):
        send_own(CODE_B, 1, codes_v[r].at[parity, own_slot(r)], codes_v[r], 0, r)
    for copy in token_copies + attention_copies:
        copy.wait()
    for copy in weight_copies:
        copy.start()
    lax.fori_loop(0, heads // 2, split_heads, 0, unroll=8)

    lax.fori_loop(0, ATTEND[0], attend, 0, unroll=True)

    for wave in range(WAVES):
        for r in (1, 2):
            here = order_of(r, digits_of(0, wave, iota((ROWS, ROWS), 0)))
            perm[wave, :, pl.ds((r - 1) * ROWS, ROWS)] = jnp.where(here == iota((ROWS, ROWS), 1), 1.0, 0.0).astype(BF16)

    lax.fori_loop(ATTEND[0], ATTEND[0] + ATTEND[1], attend, 0, unroll=True)

    def pass_on(refs, stages, wave, c, r):
        a, b, _ = ROTATIONS[r]
        mine = refs.at[wave]
        far = mine.at[slot_of(r, (me[a] + 2) % SIDE)]
        both = mine.at[rows_at(me[b], 2 * TOK)]

        @pl.when(parity == wave)
        def _():
            await_rows(mine, TOK, recv_sem, stages[0], wave, c, r)
            for k in (1, 3, 2):
                remote(far, far, stages[1], wave, c, r, device(**{b: (me[b] + k) % SIDE})).start()

        @pl.when(parity != wave)
        def _():
            await_rows(mine, 2 * TOK, recv_sem, stages[0], wave, c, r)
            for k in (1, 3, 2):
                remote(both, both, stages[1], wave, c, r, device(**{b: (me[b] + k) % SIDE})).start()

    for wave in range(WAVES):
        for c, r in PARTS:
            pass_on(held[c][r], (GATHER_A, GATHER_B), wave, c, r)
        for r in range(3):
            pass_on(codes_v[r], (CODE_A, CODE_B), wave, 0, r)
        if wave == 0:
            lax.fori_loop(ATTEND[0] + ATTEND[1], sum(ATTEND), attend, 0, unroll=True)

    place = iota((BLOCK, HELD), 0)
    own_source = place % FEW == iota((BLOCK, HELD), 1) // TOK
    slot_sign = jnp.where(place < FEW, 1.0, -1.0)
    line_order = ((1, 0), (3, 1), (2, 0), (3, 0), (1, 1), (2, 1), (0, 1))

    def own_block(r):
        return rows_at(me[ROTATIONS[r][2]] * 2 + me["core"], BLOCK)

    def line_peer(r, k, flip):
        c_axis = ROTATIONS[r][2]
        at, core = (me[c_axis] + k) % SIDE, (me["core"] + flip) % 2
        return rows_at(at * 2 + core, BLOCK), device(**{c_axis: at, "core": core})

    def exchange(outgoing, incoming, stage, wave, c, r):
        for k, flip in line_order:
            block, to = line_peer(r, k, flip)
            remote(outgoing.at[block], incoming.at[own_block(r)], stage, wave, c, r, to).start()
        incoming[own_block(r), :] = outgoing[own_block(r), :]

    scaled = {}
    for wave in range(WAVES):
        pick = []
        for r in range(3):
            await_rows(codes_v[r].at[wave], 6 * TOK, recv_sem, CODE_B, wave, 0, r)
            c_axis = ROTATIONS[r][2]
            peer = iota((LINE, LANE), 0)
            at = dict(me)
            at[c_axis] = peer // 2
            expert = (at["z"] * 2 + peer % 2) * 16 + at["x"] * 4 + at["y"]
            select = jnp.where(expert == iota((LINE, LANE), 1), 1.0, 0.0).astype(BF16)
            codes = dot_nt(select, codes_v[r][wave])
            parts = []
            for e in range(LINE):
                signed = codes[e : e + 1, :] * slot_sign
                parts.append(jnp.where(jnp.logical_and(own_source, signed > 0.0), signed, 0.0))
            scaled[wave, r] = jnp.concatenate(parts, axis=0)
            pick.append(jnp.where(scaled[wave, r] > 0.0, 1.0, 0.0).astype(BF16))
        for c in range(CHUNKS):
            for r in range(3):
                await_rows(held[c][r].at[wave], 6 * TOK, recv_sem, GATHER_B, wave, c, r)
            for r in range(3):
                send[wave][c][r][...] = dot(pick[r], held[c][r][wave]).astype(BF16)
            for r in range(3):
                exchange(send[wave][c][r], recv[wave][c][r], TO_EXPERT, wave, c, r)
    for wave in range(WAVES):
        for r in range(3):
            weigh[wave, r] = scaled[wave, r].T.astype(BF16)

    pair = 2 * TOK

    def combine(wave, c, r):
        b = ROTATIONS[r][1]
        await_rows(back[wave][c][r], ROWS - BLOCK, recv_sem, FROM_EXPERT, wave, c, r)
        mine = part[wave][c][r]
        mine[...] = dot(weigh[wave, r], back[wave][c][r][...]).astype(BF16)
        own = rows_at(me[b], pair)
        for k in (1, 3, 2):
            to = (me[b] + k) % SIDE
            remote(mine.at[rows_at(to, pair)], sum_b[wave][c][r].at[own], SUM_B, wave, c, r, device(**{b: to})).start()
        sum_b[wave][c][r][own, :] = mine[own, :]

    ff = gate_v.shape[1]
    step = 512
    for wave in range(WAVES):
        for c, r in PARTS:
            await_rows(recv[wave][c][r], ROWS - BLOCK, recv_sem, TO_EXPERT, wave, c, r)
        for c, r in PARTS:
            start, width = COLS[c][r]
            if r == 0:
                aligned[:, pl.ds(start, width)] = recv[wave][c][r][...]
            else:
                aligned[:, pl.ds(start, width)] = dot(perm[wave, :, pl.ds((r - 1) * ROWS, ROWS)], recv[wave][c][r][...]).astype(BF16)
        if wave == 0:
            for copy in weight_copies:
                copy.wait()

        def ff_tile(n, _):
            tile = pl.ds(pl.multiple_of(n * step, step), step)
            gate = dot(aligned[...], gate_v[:, tile])
            upper = dot(aligned[...], up_v[:, tile])
            hidden[:, tile] = (gate / (1.0 + jnp.exp(-gate)) * upper).astype(BF16)
            return 0

        lax.fori_loop(0, ff // step, ff_tile, 0, unroll=True)
        for c, r in PARTS:
            start, width = COLS[c][r]
            if r == 1 and c == 0:
                hidden_r[...] = lax.dot_general(
                    perm[wave], hidden[...], (((0,), (0,)), ((), ())), preferred_element_type=F32
                ).astype(BF16)
            rows = hidden[...] if r == 0 else hidden_r[pl.ds((r - 1) * ROWS, ROWS), :]
            result[wave][c][r][...] = dot(rows, down_v[:, pl.ds(start, width)]).astype(BF16)
            exchange(result[wave][c][r], back[wave][c][r], FROM_EXPERT, wave, c, r)
    lax.fori_loop(sum(ATTEND), seqs, attend, 0, unroll=True)
    lax.fori_loop(0, heads, join_heads, 0, unroll=8)
    attn_copy = pltpu.make_async_copy(attn_v, attn_out, local_sem.at[len(local)])
    attn_copy.start()

    for wave in range(WAVES):
        for c, r in PARTS:
            combine(wave, c, r)

    for wave in range(WAVES):
        for c, r in PARTS:
            a, b, _ = ROTATIONS[r]
            arrived = sum_b[wave][c][r]
            await_rows(arrived, 3 * pair, recv_sem, SUM_B, wave, c, r)
            total = arrived[pl.ds(0, pair), :].astype(F32)
            for k in range(1, SIDE):
                total = total + arrived[pl.ds(k * pair, pair), :].astype(F32)
            mine = both_b[wave][c][r]
            mine[...] = total.astype(BF16)
            own = rows_at(me[a], TOK)

            def give(to, c=c, r=r, wave=wave, mine=mine, own=own, a=a):
                remote(mine.at[rows_at(to // 2, TOK)], sum_a[c][r].at[own], SUM_A, wave, c, r, device(**{a: to})).start()

            @pl.when(parity == wave)
            def _():
                give((me[a] + 2) % SIDE)
                sum_a[c][r][own, :] = mine[rows_at(me[a] // 2, TOK), :]

            @pl.when(parity != wave)
            def _():
                give((me[a] + 1) % SIDE)
                give((me[a] + 3) % SIDE)

    for c, r in PARTS:
        start, width = COLS[c][r]
        await_rows(sum_a[c][r], 3 * TOK, recv_sem, SUM_A, parity, c, r)
        total = sum_a[c][r][pl.ds(0, TOK), :].astype(F32)
        for k in range(1, SIDE):
            total = total + sum_a[c][r][pl.ds(k * TOK, TOK), :].astype(F32)
        moe_v[:, pl.ds(start, width)] = total.astype(BF16)
    moe_copy = pltpu.make_async_copy(moe_v, moe_out, local_sem.at[len(local) + 1])
    moe_copy.start()

    for c, r in PARTS:
        await_rows(held[c][r].at[0], 3 * TOK, send_sem, GATHER_A, parity, c, r)
        if c == 0:
            await_rows(codes_v[r].at[0], 3 * TOK, send_sem, CODE_A, parity, 0, r)
        for wave in range(WAVES):
            if c == 0:
                await_rows(codes_v[r].at[wave], 6 * TOK, send_sem, CODE_B, wave, 0, r)
            await_rows(back[wave][c][r], ROWS - BLOCK, send_sem, TO_EXPERT, wave, c, r)
            await_rows(back[wave][c][r], ROWS - BLOCK, send_sem, FROM_EXPERT, wave, c, r)
            await_rows(sum_b[wave][c][r], 3 * pair, send_sem, SUM_B, wave, c, r)
            await_rows(held[c][r].at[wave], 6 * TOK, send_sem, GATHER_B, wave, c, r)

            @pl.when(parity == wave)
            def _():
                await_rows(sum_a[c][r], TOK, send_sem, SUM_A, wave, c, r)

            @pl.when(parity != wave)
            def _():
                await_rows(sum_a[c][r], 2 * TOK, send_sem, SUM_A, wave, c, r)
    attn_copy.wait()
    moe_copy.wait()


def per_device(tokens, routes, affinity, w_gate, w_up, w_down, q_latent, q_rope, cache_latent, cache_rope, lengths):
    tok_dev, width = tokens.shape
    ff = w_gate.shape[2]
    seqs, heads, latent = q_latent.shape

    def buffers(rows):
        return [pltpu.VMEM((rows, COLS[c][r][1]), BF16) for c, r in PARTS]

    scratch = (
        [pltpu.VMEM((WAVES, HELD, COLS[c][r][1]), BF16) for c, r in PARTS]
        + buffers(ROWS) * (4 * WAVES)
        + buffers(HELD) * (2 * WAVES)
        + buffers(2 * TOK) * WAVES
        + buffers(SIDE * TOK)
        + [pltpu.VMEM((WAVES, HELD, LANE), BF16)] * 3
        + [
            pltpu.VMEM((ROWS, width), BF16),
            pltpu.VMEM((ROWS, ff), BF16),
            pltpu.VMEM((2 * ROWS, ff), BF16),
            pltpu.VMEM((WAVES, 3, HELD, ROWS), BF16),
            pltpu.VMEM((WAVES, ROWS, 2 * ROWS), BF16),
            pltpu.VMEM(routes.shape[::-1], jnp.int32),
            pltpu.VMEM(affinity.shape[::-1], F32),
            pltpu.VMEM((width, ff), BF16),
            pltpu.VMEM((width, ff), BF16),
            pltpu.VMEM((ff, width), BF16),
            pltpu.VMEM(q_latent.shape, BF16),
            pltpu.VMEM(q_rope.shape, BF16),
            pltpu.VMEM(cache_latent.shape, BF16),
            pltpu.VMEM(cache_rope.shape, BF16),
            pltpu.SMEM(lengths.shape, jnp.int32),
            pltpu.VMEM((seqs * heads, LANE), F32),
            pltpu.VMEM((latent // LANE, seqs * heads, LANE), F32),
            pltpu.VMEM((seqs, heads * latent), BF16),
            pltpu.VMEM((tok_dev, width), BF16),
            pltpu.SemaphoreType.DMA((STAGES, WAVES, len(PARTS))),
            pltpu.SemaphoreType.DMA((STAGES, WAVES, len(PARTS))),
            pltpu.SemaphoreType.DMA((2 + len(PARTS) + 5 + 2,)),
            pltpu.SemaphoreType.DMA((3,)),
        ]
    )
    results = pl.pallas_call(
        kernel,
        out_shape=(
            jax.ShapeDtypeStruct((tok_dev, width), BF16),
            jax.ShapeDtypeStruct((seqs, heads * latent), BF16),
        ),
        in_specs=[pl.BlockSpec(memory_space=pl.ANY)] * 11,
        out_specs=[pl.BlockSpec(memory_space=pl.ANY)] * 2,
        scratch_shapes=scratch,
        compiler_params=pltpu.CompilerParams(
            collective_id=0, has_side_effects=True, vmem_limit_bytes=62 * 1024 * 1024
        ),
    )(tokens, routes.T, affinity.T, w_gate, w_up, w_down, q_latent, q_rope, cache_latent, cache_rope, lengths)
    anywhere = [pl.BlockSpec(memory_space=pl.ANY)] * 2
    return pl.pallas_call(
        finish,
        out_shape=tuple(jax.ShapeDtypeStruct(x.shape, x.dtype) for x in results),
        in_specs=anywhere,
        out_specs=anywhere,
        scratch_shapes=[pltpu.VMEM(x.shape, x.dtype) for x in results]
        + [pltpu.SemaphoreType.DMA((3,)), pltpu.SemaphoreType.DMA((3,))],
        compiler_params=pltpu.CompilerParams(vmem_limit_bytes=62 * 1024 * 1024),
    )(*results)


def finish(moe_in, attn_in, moe_out, attn_out, moe_v, attn_v, in_sem, out_sem):
    half = attn_in.shape[1] // 2
    pieces = [(moe_in, moe_v, moe_out)]
    for i in range(2):
        pieces.append(tuple(ref.at[:, pl.ds(i * half, half)] for ref in (attn_in, attn_v, attn_out)))
    first = [pltpu.make_async_copy(src, mid, in_sem.at[i]) for i, (src, mid, _) in enumerate(pieces)]
    last = [pltpu.make_async_copy(mid, dst, out_sem.at[i]) for i, (_, mid, dst) in enumerate(pieces)]
    for copy in first:
        copy.start()
    for copy, then in zip(first, last):
        copy.wait()
        then.start()
    for copy in last:
        copy.wait()


def solution(mesh):
    rows = P(("group", "member"), None)
    cube = P(("group", "member"), None, None)
    return jax.shard_map(
        per_device,
        mesh=mesh,
        in_specs=(rows, rows, rows, cube, cube, cube, cube, rows, cube, cube, P(("group", "member"))),
        out_specs=(rows, rows),
        check_vma=False,
    )
```
